256 devices in a mesh: dp: 16 (over y, z_hi, core), section: 4 (over z_lo), tensor: 4 (over x).
Axes of the slice: x: 4, y: 4, z: 8 (z_hi: 2, z_lo: 4; z = z_hi * 4 + z_lo), core: 2. Of those that a mesh axis runs over, the one named last changes fastest.
Arguments:
- upstream_derivative: bfloat16 [4, 512, 8192], P(None, 'dp', 'tensor'), may hold values from -6 to 6
- stored_level_activations: bfloat16 [4, 4, 512, 8192], P('section', None, 'dp', 'tensor'), may hold values from -6 to 6
- fixed_projection_matrix: bfloat16 [4, 8192, 8192], P('section', 'tensor', 'dp'), may hold values from -0.0625 to 0.0625
- lowrank_left_matrices: bfloat16 [4, 8192, 256], P('section', 'tensor'), may hold values from -0.0625 to 0.0625
- lowrank_right_matrices: bfloat16 [4, 256, 8192], P('section', None, 'tensor'), may hold values from -0.0625 to 0.0625
- mixture_coefficients: float32 [4, 512, 64], P(None, 'dp', 'section'), may hold values from 0.05 to 1
- classifier_feature_states: bfloat16 [4, 512, 8192], P(None, 'dp', 'tensor'), may hold values from -6 to 6
- classifier_matrix: float32 [8192, 64], P('tensor', 'section'), may hold values from -0.75 to 0.75
Outputs:
- input_grads: bfloat16 [4, 4, 512, 8192], P('section', None, 'dp', 'tensor')
- scale_grads: float32 [4, 512, 64], P(None, 'dp', 'section')
- head_grad: float32 [8192, 64], P('tensor', 'section')
- hidden_grad: float32 [4, 512, 8192], P(None, 'dp', 'tensor')
The draws below stay inside these ranges and needn't reach their ends.
All inputs are finite; a program needn't handle non-finite values.
Results may differ from the reference program's by a relative error of at most 0.008.
Values may be sent and summed in bfloat16 or wider, within the bound.
A program may use at most 128 MiB of HBM per device.

```python
import math
import jax
import jax.numpy as jnp
from jax import lax

D = 8192
SPECIALIST_TALLY = 16
RANK = 16
MINIBATCH_GROUPS = 4
LAYERS = 4
SEQUENCE_SPAN = 512
TOKENS = 2048
MIXING_TALLY = 64


def steps_of(own_key, extent, cuts, smallest, top_value):
    factor_of = 1.0
    for position, parts in cuts:
        steps = jax.random.uniform(jax.random.fold_in(jax.random.fold_in(own_key, 6), position), (parts,), jnp.float32, smallest / len(cuts), top_value / len(cuts))
        factor_of = factor_of * jnp.repeat(jnp.exp(steps), extent[position] // parts).reshape((-1,) + (1,) * (len(extent) - 1 - position))
    return factor_of


def noise(key, extent, spread, most, split=(), dtype=jnp.bfloat16):
    level = steps_of(key, extent, split, -0.22, 0.18) if split else 1.0
    values = jax.random.normal(key, extent, jnp.float32) * spread * level
    return jnp.minimum(jnp.maximum(values, -most), most).astype(dtype)


def setup_inputs(seed: int = 0) -> dict:
    seeds = jax.random.split(jax.random.key(seed), 9)
    return {
        "upstream_derivative": noise(seeds[0], (MINIBATCH_GROUPS, SEQUENCE_SPAN, D), 1.0, 6.0, ((1, 16), (2, 4))),
        "stored_level_activations": noise(seeds[1], (LAYERS, MINIBATCH_GROUPS, SEQUENCE_SPAN, D), 1.0, 6.0, ((0, 4), (2, 16), (3, 4))),
        "fixed_projection_matrix": noise(seeds[2], (LAYERS, D, D), D ** -0.5, 0.0625, ((0, 4), (1, 4), (2, 16))),
        "lowrank_left_matrices": noise(seeds[3], (LAYERS, D, SPECIALIST_TALLY * RANK), D ** -0.5, 0.0625, ((0, 4), (1, 4))),
        "lowrank_right_matrices": noise(seeds[4], (LAYERS, SPECIALIST_TALLY * RANK, D), D ** -0.5, 0.0625, ((0, 4), (2, 4))),
        "mixture_coefficients": jnp.clip(0.05 + 0.95 * jax.random.uniform(seeds[5], (MINIBATCH_GROUPS, SEQUENCE_SPAN, MIXING_TALLY), jnp.float32) ** steps_of(seeds[5], (MINIBATCH_GROUPS, SEQUENCE_SPAN, MIXING_TALLY), ((1, 16), (2, 4)), -0.2, 0.2), 0.05, 1.0),
        "classifier_feature_states": noise(seeds[6], (MINIBATCH_GROUPS, SEQUENCE_SPAN, D), 1.0, 6.0, ((1, 16), (2, 4))),
        "classifier_matrix": noise(seeds[7], (D, MIXING_TALLY), MIXING_TALLY ** -0.5, 0.75, ((0, 4), (1, 4)), jnp.float32),
    }


def reference(upstream_derivative, stored_level_activations, fixed_projection_matrix, lowrank_left_matrices, lowrank_right_matrices, mixture_coefficients, classifier_feature_states, classifier_matrix):
    incoming = upstream_derivative.reshape(MINIBATCH_GROUPS * SEQUENCE_SPAN, D)
    grads_list = []
    scale_list = []
    for depth_ordinal in reversed(range(LAYERS)):
        hidden = stored_level_activations[depth_ordinal].reshape(MINIBATCH_GROUPS * SEQUENCE_SPAN, D)
        base = jnp.dot(incoming, fixed_projection_matrix[depth_ordinal], preferred_element_type=jnp.float32)
        back = jnp.dot(incoming, lowrank_right_matrices[depth_ordinal].T, preferred_element_type=jnp.float32)
        down = jnp.dot(hidden, lowrank_left_matrices[depth_ordinal], preferred_element_type=jnp.float32)
        sgrad = (down * back).reshape(-1, SPECIALIST_TALLY, RANK).sum(axis=-1)
        mixing_coefficient = mixture_coefficients[:, :, depth_ordinal * SPECIALIST_TALLY:(depth_ordinal + 1) * SPECIALIST_TALLY].reshape(-1, SPECIALIST_TALLY)
        weighted = (back.reshape(-1, SPECIALIST_TALLY, RANK) * mixing_coefficient[:, :, None]).reshape(-1, SPECIALIST_TALLY * RANK).astype(jnp.bfloat16)
        adapter = jnp.dot(weighted, lowrank_left_matrices[depth_ordinal].T, preferred_element_type=jnp.float32)
        incoming = (incoming.astype(jnp.float32) + base + adapter).astype(jnp.bfloat16)
        grads_list.insert(0, incoming.reshape(MINIBATCH_GROUPS, SEQUENCE_SPAN, D))
        scale_list.insert(0, sgrad.reshape(MINIBATCH_GROUPS, SEQUENCE_SPAN, SPECIALIST_TALLY))
    input_grads = jnp.stack(grads_list, axis=0)
    scale_grads = jnp.concatenate(scale_list, axis=2)
    flat_scales = scale_grads.reshape(-1, MIXING_TALLY)
    states = classifier_feature_states.reshape(-1, D).astype(jnp.float32)
    head_grad = jnp.dot(states.T, flat_scales, precision=lax.Precision.HIGHEST) * (1.0 / math.sqrt(TOKENS))
    hidden_grad = jnp.dot(flat_scales, classifier_matrix.T, precision=lax.Precision.HIGHEST).reshape(MINIBATCH_GROUPS, SEQUENCE_SPAN, D)
    return (input_grads, scale_grads, head_grad, hidden_grad)
```

```python
import functools
import math

import jax
import jax.numpy as jnp
from jax import lax
from jax.experimental import pallas as pl
from jax.experimental.pallas import tpu as pltpu
from jax.sharding import PartitionSpec as P

BF = jnp.bfloat16
F32 = jnp.float32
NT_DIMS = (((1,), (1,)), ((), ()))
SUBS = 4
TOK = 16


def dot_nt(a, b, precision=None):
    return lax.dot_general(a, b, NT_DIMS, precision=precision, preferred_element_type=F32)


def kernel(
    sizes,
    u, hid, w, a, b, st, states, ct,
    out, scale, head, hidden,
    g, pb, rx, own, sp, se, sb, sall, ai, dx, bx, pacc, bacc, cta, sga, hl, hx, ho,
    r_s, r_z, r_y, r_c, r_x,
    s_s, s_z, s_c, s_x, s_p, s_o, s_b, s_u,
    r_one, s_one,
):
    X, Y, S, DP, N, R = sizes
    T = TOK
    FB = w.shape[1]
    ex = scale.shape[1]
    rank = R // ex
    d = lax.axis_index("dp")
    sec = lax.axis_index("section")
    x = lax.axis_index("tensor")
    y = d // SUBS
    m = d % SUBS
    zh = m // 2
    core = m % 2

    def dev(dp=None, section=None, tensor=None):
        return {
            "dp": d if dp is None else dp,
            "section": sec if section is None else section,
            "tensor": x if tensor is None else tensor,
        }

    def send(src, dst, ssem, rsem, target):
        pltpu.make_async_remote_copy(
            src_ref=src, dst_ref=dst, send_sem=ssem, recv_sem=rsem,
            device_id=target, device_id_type=pl.DeviceIdType.MESH,
        ).start()

    def wait(ref, sem):
        pltpu.make_async_copy(ref, ref, sem).wait()

    def cols(index, width):
        return pl.ds(pl.multiple_of(index * width, 128), width)

    def rows(index, height):
        return pl.ds(pl.multiple_of(index * height, 16), height)

    same = x == y
    apart = jnp.logical_not(same)
    top = sec == S - 1
    bottom = sec == 0

    barrier = pltpu.get_barrier_semaphore()

    def hello(target):
        pl.semaphore_signal(barrier, inc=1, device_id=target, device_id_type=pl.DeviceIdType.MESH)

    for j in range(1, DP):
        hello(dev(dp=(d + j) % DP))
    for j in range(1, X):
        hello(dev(tensor=(x + j) % X))
    for j in range(1, S):
        hello(dev(section=(sec + j) % S))

    @pl.when(apart)
    def _():
        for o in range(SUBS):
            hello(dev(dp=x * SUBS + o, tensor=y))

        @pl.when(sec > 0)
        def _():
            hello(dev(dp=x * SUBS + m, section=sec - 1, tensor=y))

        @pl.when(sec < S - 1)
        def _():
            hello(dev(dp=x * SUBS + m, section=sec + 1, tensor=y))

    extra = SUBS + jnp.where(bottom, 0, 1) + jnp.where(top, 0, 1)
    pl.semaphore_wait(barrier, DP - 1 + X - 1 + S - 1 + jnp.where(same, 0, extra))

    @pl.when(top)
    def _():
        @pl.loop(0, N)
        def _(k):
            for j in range(1, SUBS):
                o = (m + j) % SUBS
                send(u.at[k, :, cols(o, FB)], g.at[k, o % 2, y, o // 2, m],
                     s_u.at[k], r_s.at[k], dev(dp=y * SUBS + o))
            pltpu.make_async_copy(u.at[k, :, cols(m, FB)], g.at[k, core, y, zh, m], r_s.at[k]).start()

    s_full = st[...]
    s_hi = s_full.astype(BF)
    s_lo = (s_full - s_hi.astype(F32)).astype(BF)
    both = jnp.concatenate([s_hi, s_lo], axis=0)
    sb[...] = both
    sall[d] = both
    for j in range(1, DP):
        send(sb, sall.at[d], s_one.at[0], r_one.at[0], dev(dp=(d + j) % DP))

    @pl.when(apart)
    def _():
        send(a.at[rows(m, FB)], ai, s_one.at[1], r_one.at[1], dev(dp=x * SUBS + m, tensor=y))

    @pl.when(same)
    def _():
        pltpu.make_async_copy(a.at[rows(m, FB)], ai, r_one.at[1]).start()

    cta[sec] = ct[...]
    for j in range(1, S):
        send(ct, cta.at[sec], s_one.at[2], r_one.at[2], dev(section=(sec + j) % S))

    def step_s(k):
        mine = g.at[k, core, y, zh]
        wait(mine, r_s.at[k])
        send(mine, mine, s_s.at[k], r_z.at[k], dev(dp=(d + 2) % SUBS + y * SUBS))
        for j in range(1, Y):
            send(mine, mine, s_s.at[k], r_y.at[k], dev(dp=((y + j) % Y) * SUBS + m))

    def step_z(k):
        theirs = g.at[k, core, y, 1 - zh]
        wait(theirs, r_z.at[k])
        for j in range(1, Y):
            send(theirs, theirs, s_z.at[k], r_y.at[k], dev(dp=((y + j) % Y) * SUBS + m))

    def prepare():
        down = jnp.dot(hid[...], a[...], preferred_element_type=F32)
        dx[x] = down
        for j in range(1, X):
            send(dx.at[x], dx.at[x], s_one.at[3], r_one.at[3], dev(tensor=(x + j) % X))
        wait(sall.at[pl.ds(0, DP - 1)], r_one.at[0])
        expert = lax.broadcasted_iota(jnp.int32, (2 * ex, R), 0)
        column = lax.broadcasted_iota(jnp.int32, (2 * ex, R), 1)
        expand = jnp.where(lax.rem(expert, ex) == lax.div(column, rank), 1.0, 0.0).astype(BF)

        @pl.loop(0, DP)
        def _(owner):
            turned = sall[owner].astype(F32).T.astype(BF)
            se[owner] = jnp.dot(turned, expand, preferred_element_type=F32)

        wait(ai, r_one.at[1])

    def half(k, c):
        total = None
        back = None
        for zz in range(2):
            f = zz * 2 + c
            left = g[k, c, :, zz].reshape(Y * SUBS * T, FB)
            t = jnp.dot(left, w[rows(f, FB), :], preferred_element_type=F32)
            q = dot_nt(left, b[:, cols(f, FB)])
            total = t if total is None else total + t
            back = q if back is None else back + q
        return total, back

    def step_m(k):
        wait(g.at[k, 0, pl.ds(0, Y - 1)], r_y.at[k])
        send(g.at[k, core], g.at[k, core], s_c.at[k], r_c.at[k], dev(dp=d + 1 - 2 * core))
        total, back = half(k, core)
        pacc[...] = total
        bacc[...] = back
        wait(g.at[k, 0], r_c.at[k])

        @pl.when(sec < S - 1)
        def _():
            send(g.at[k, :, y, :, m], out.at[k], s_o.at[k], r_one.at[4], dev(section=sec + 1))

        total, back = half(k, 1 - core)
        back = bacc[...] + back
        bacc[...] = back
        spread = se[:, rows(k, T), :].reshape(DP * T, R)
        weighted = (back * spread).astype(BF)
        pacc[...] += total + dot_nt(weighted, ai[...])

        @pl.when(same)
        def _():
            pacc[...] += g[k, core, :, zh].reshape(Y * SUBS * T, FB).astype(F32)

        pb[k] = pacc[...].astype(BF).reshape(Y, SUBS, T, FB)
        for j in range(1, X):
            r = (x + j) % X
            send(pb.at[k, r], rx.at[k, x], s_x.at[k], r_x.at[k], dev(tensor=r))
        own[k] = pacc[rows(x, SUBS * T), :]
        bx[x, k] = bacc[rows(d, T), :]
        for j in range(1, X):
            send(bx.at[x, k], bx.at[x, k], s_b.at[k], r_one.at[5], dev(tensor=(x + j) % X))

    def step_x(k):
        wait(rx.at[k, pl.ds(0, X - 1)], r_x.at[k])
        total = own[k]
        for j in range(1, X):
            total = total + rx[k, (x + j) % X].reshape(SUBS * T, FB).astype(F32)
        sp[k] = total.astype(BF).reshape(SUBS, T, FB)

        @pl.when(sec > 0)
        def _():
            send(sp.at[k], g.at[k, core, x, zh], s_p.at[k], r_s.at[k],
                 dev(dp=x * SUBS + m, section=sec - 1, tensor=y))

        @pl.when(bottom)
        def _():
            for o in range(SUBS):
                here = jnp.logical_and(same, m == o)

                @pl.when(here)
                def _():
                    pltpu.make_async_copy(sp.at[k, o], out.at[k, core, zh], r_one.at[4]).start()

                @pl.when(jnp.logical_not(here))
                def _():
                    send(sp.at[k, o], out.at[k, core, zh], s_p.at[k], r_one.at[4],
                         dev(dp=x * SUBS + o, tensor=y))

    @pl.loop(0, N + 2)
    def _(i):
        @pl.when(i < N)
        def _():
            step_s(i)

        @pl.when(i >= 2)
        def _():
            step_x(i - 2)

        @pl.when(i < N)
        def _():
            step_z(i)

        @pl.when(i == 1)
        def _():
            prepare()

        @pl.when(jnp.logical_and(i >= 1, i < N + 1))
        def _():
            step_m(i - 1)

    wait(bx.at[pl.ds(0, X - 1)], r_one.at[5])
    wait(dx.at[pl.ds(0, X - 1)], r_one.at[3])
    back = bx[0].reshape(N * T, R)
    down = dx[0]
    for j in range(1, X):
        back = back + bx[j].reshape(N * T, R)
        down = down + dx[j]
    product = down * back
    expert = lax.broadcasted_iota(jnp.int32, (ex, R), 0)
    column = lax.broadcasted_iota(jnp.int32, (ex, R), 1)
    group = jnp.where(expert == lax.div(column, rank), 1.0, 0.0).astype(F32)
    scale[...] = dot_nt(product, group, lax.Precision.HIGHEST)
    turned = dot_nt(group, product, lax.Precision.HIGHEST)
    sga[sec] = turned
    for j in range(1, S):
        send(sga.at[sec], sga.at[sec], s_one.at[5], r_one.at[6], dev(section=(sec + j) % S))

    t_hi = turned.astype(BF)
    t_lo = (turned - t_hi.astype(F32)).astype(BF)
    hl[...] = (jnp.dot(t_hi, states[...], preferred_element_type=F32)
               + jnp.dot(t_lo, states[...], preferred_element_type=F32))
    FD = hl.shape[1] // DP
    for j in range(1, DP):
        e = (d + j) % DP
        send(hl.at[:, cols(e, FD)], hx.at[d], s_one.at[6], r_one.at[7], dev(dp=e))
    hx[d] = hl[:, cols(d, FD)]
    wait(hx.at[pl.ds(0, DP - 1)], r_one.at[7])
    total = hx[0]
    for j in range(1, DP):
        total = total + hx[j]
    total = total * (1.0 / math.sqrt(N * T * DP))
    ho[...] = total
    head[:, cols(d, FD)] = total
    for j in range(1, DP):
        send(ho, head.at[:, cols(d, FD)], s_one.at[7], r_one.at[8], dev(dp=(d + j) % DP))

    wait(cta.at[pl.ds(0, S - 1)], r_one.at[2])
    wait(sga.at[pl.ds(0, S - 1)], r_one.at[6])
    left = sga[...].reshape(S * ex, N * T).T
    right = cta[...].reshape(S * ex, -1)
    hidden[...] = jnp.dot(left, right, precision=lax.Precision.HIGHEST, preferred_element_type=F32)

    wait(hx.at[pl.ds(0, DP - 1)], r_one.at[8])
    wait(out, r_one.at[4])
    wait(sall.at[pl.ds(0, DP - 1)], s_one.at[0])

    @pl.when(apart)
    def _():
        wait(ai, s_one.at[1])

    wait(cta.at[pl.ds(0, S - 1)], s_one.at[2])
    wait(dx.at[pl.ds(0, X - 1)], s_one.at[3])
    wait(sga.at[pl.ds(0, S - 1)], s_one.at[5])
    wait(hx.at[pl.ds(0, DP - 1)], s_one.at[6])
    wait(hx.at[pl.ds(0, DP - 1)], s_one.at[7])

    @pl.loop(0, N)
    def _(k):
        wait(g.at[k, 0, :, 0], s_s.at[k])
        wait(g.at[k, 0, pl.ds(0, Y - 1), 0], s_z.at[k])
        wait(g.at[k, 0], s_c.at[k])
        wait(rx.at[k, pl.ds(0, X - 1)], s_x.at[k])
        wait(bx.at[pl.ds(0, X - 1), k], s_b.at[k])

        @pl.when(top)
        def _():
            wait(sp.at[k, pl.ds(0, SUBS - 1)], s_u.at[k])

        @pl.when(sec > 0)
        def _():
            wait(sp.at[k], s_p.at[k])

        @pl.when(jnp.logical_and(bottom, apart))
        def _():
            wait(sp.at[k], s_p.at[k])

        @pl.when(jnp.logical_and(bottom, same))
        def _():
            wait(sp.at[k, pl.ds(0, SUBS - 1)], s_p.at[k])

        @pl.when(sec < S - 1)
        def _():
            wait(out.at[k], s_o.at[k])


def on_device(u, saved, w, a, b, mix, states, classifier):
    X, S, DP = (lax.axis_size(n) for n in ("tensor", "section", "dp"))
    Y = DP // SUBS
    micro, per, F = u.shape
    T = TOK
    N = micro * per // T
    FB = w.shape[2]
    R = a.shape[2]
    ex = mix.shape[2]
    tokens = N * T
    vmem = pl.BlockSpec(memory_space=pltpu.VMEM)
    dma = pltpu.SemaphoreType.DMA
    sizes = (X, Y, S, DP, N, R)
    out, scale, head, hidden = pl.pallas_call(
        functools.partial(kernel, sizes),
        out_shape=(
            jax.ShapeDtypeStruct((N, 2, 2, T, FB), BF),
            jax.ShapeDtypeStruct((tokens, ex), F32),
            jax.ShapeDtypeStruct((ex, F), F32),
            jax.ShapeDtypeStruct((tokens, F), F32),
        ),
        in_specs=[vmem] * 8,
        out_specs=(vmem,) * 4,
        scratch_shapes=[
            pltpu.VMEM((N, 2, Y, 2, SUBS, T, FB), BF),
            pltpu.VMEM((N, Y, SUBS, T, FB), BF),
            pltpu.VMEM((N, X, SUBS, T, FB), BF),
            pltpu.VMEM((N, SUBS * T, FB), F32),
            pltpu.VMEM((N, SUBS, T, FB), BF),
            pltpu.VMEM((DP, tokens, R), F32),
            pltpu.VMEM((2 * ex, tokens), BF),
            pltpu.VMEM((DP, 2 * ex, tokens), BF),
            pltpu.VMEM((FB, R), BF),
            pltpu.VMEM((X, tokens, R), F32),
            pltpu.VMEM((X, N, T, R), F32),
            pltpu.VMEM((Y * SUBS * T, FB), F32),
            pltpu.VMEM((Y * SUBS * T, R), F32),
            pltpu.VMEM((S, ex, F), F32),
            pltpu.VMEM((S, ex, tokens), F32),
            pltpu.VMEM((ex, F), F32),
            pltpu.VMEM((DP, ex, F // DP), F32),
            pltpu.VMEM((ex, F // DP), F32),
        ] + [dma((N,))] * 13 + [dma((9,)), dma((8,))],
        compiler_params=pltpu.CompilerParams(
            collective_id=0, has_side_effects=True, vmem_limit_bytes=48 * 1024 * 1024,
        ),
    )(
        u.reshape(N, T, F),
        saved.reshape(tokens, F),
        w[0], a[0], b[0],
        mix.reshape(tokens, ex).T,
        states.reshape(tokens, F),
        classifier.T,
    )
    grads = out.reshape(micro, per // T, 2, 2, T, FB).transpose(0, 1, 4, 3, 2, 5).reshape(1, micro, per, F)
    return grads, scale.reshape(micro, per, ex), head.T, hidden.reshape(micro, per, F)


def solution(mesh):
    return jax.shard_map(
        on_device,
        mesh=mesh,
        in_specs=(
            P(None, "dp", "tensor"),
            P("section", None, "dp", "tensor"),
            P("section", "tensor", "dp"),
            P("section", "tensor", None),
            P("section", None, "tensor"),
            P(None, "dp", "section"),
            P(None, "dp", "tensor"),
            P("tensor", "section"),
        ),
        out_specs=(
            P("section", None, "dp", "tensor"),
            P(None, "dp", "section"),
            P("tensor", "section"),
            P(None, "dp", "tensor"),
        ),
        check_vma=False,
    )
```

```python
import functools
import math

import jax
import jax.numpy as jnp
from jax import lax
from jax.experimental import pallas as pl
from jax.experimental.pallas import tpu as pltpu
from jax.sharding import PartitionSpec as P

BF = jnp.bfloat16
F32 = jnp.float32
NT_DIMS = (((1,), (1,)), ((), ()))
SUBS = 4
TOK = 16
OWNERS = 2
ORDER = (("S", 0), ("M", 3), ("Z", 1), ("X", 4))


def dot_nt(a, b, precision=None):
    return lax.dot_general(a, b, NT_DIMS, precision=precision, preferred_element_type=F32)


def kernel(
    sizes,
    u, hid_in, w_in, a_in, b_in, mix_in, states_in, ct,
    out, scale, head, hidden,
    uv, us, hid, w, a, b, mix, states,
    g, pb, rx, own, sp, se, sb, sall, ai, dx, bx, pacc, bacc, cta, sga, hl, hx, hg,
    r_s, r_z, r_y, r_c, r_x,
    s_s, s_z, s_c, s_x, s_p, s_o, s_b, s_u,
    r_one, s_one, l_one,
):
    X, Y, S, DP, N, R = sizes
    T = TOK
    FB = w.shape[1]
    ex = mix.shape[1]
    rank = R // ex
    parts = SUBS // OWNERS
    d = lax.axis_index("dp")
    sec = lax.axis_index("section")
    x = lax.axis_index("tensor")
    y = d // SUBS
    m = d % SUBS
    zh = m // 2
    core = m % 2
    place = m % OWNERS

    def dev(dp=None, section=None, tensor=None):
        return {
            "dp": d if dp is None else dp,
            "section": sec if section is None else section,
            "tensor": x if tensor is None else tensor,
        }

    def send(src, dst, ssem, rsem, target):
        pltpu.make_async_remote_copy(
            src_ref=src, dst_ref=dst, send_sem=ssem, recv_sem=rsem,
            device_id=target, device_id_type=pl.DeviceIdType.MESH,
        ).start()

    def wait(ref, sem):
        pltpu.make_async_copy(ref, ref, sem).wait()

    def cols(index, width):
        return pl.ds(pl.multiple_of(index * width, 128), width)

    def rows(index, height):
        return pl.ds(pl.multiple_of(index * height, 16), height)

    def mine(k):
        return m // OWNERS == k % parts

    same = x == y
    apart = jnp.logical_not(same)
    top = sec == S - 1
    bottom = sec == 0

    @pl.when(top)
    def _():
        pltpu.make_async_copy(u, uv, l_one.at[6]).start()

    loads = ((mix_in, mix), (w_in, w), (b_in, b), (hid_in, hid), (a_in, a), (states_in, states))
    for i, (far, near) in enumerate(loads):
        pltpu.make_async_copy(far, near, l_one.at[i]).start()

    barrier = pltpu.get_barrier_semaphore()

    def hello(target):
        pl.semaphore_signal(barrier, inc=1, device_id=target, device_id_type=pl.DeviceIdType.MESH)

    for j in range(1, DP):
        hello(dev(dp=(d + j) % DP))
    for j in range(1, X):
        hello(dev(tensor=(x + j) % X))
    for j in range(1, S):
        hello(dev(section=(sec + j) % S))

    @pl.when(apart)
    def _():
        for o in range(SUBS):
            hello(dev(dp=x * SUBS + o, tensor=y))

        @pl.when(sec > 0)
        def _():
            hello(dev(dp=x * SUBS + m, section=sec - 1, tensor=y))

        @pl.when(sec < S - 1)
        def _():
            hello(dev(dp=x * SUBS + m, section=sec + 1, tensor=y))

    extra = SUBS + jnp.where(bottom, 0, 1) + jnp.where(top, 0, 1)
    pl.semaphore_wait(barrier, DP - 1 + X - 1 + S - 1 + jnp.where(same, 0, extra))

    @pl.when(top)
    def _():
        wait(uv, l_one.at[6])

        @pl.loop(0, N // parts)
        def _(kk):
            k = kk * parts + m // OWNERS
            for o in range(SUBS):
                us[kk, o] = uv[kk, :, o * FB:(o + 1) * FB]
            pltpu.make_async_copy(us.at[kk, m], g.at[k, core, y, zh, place], r_s.at[k]).start()
            for j in range(1, SUBS):
                o = (m + j) % SUBS
                send(us.at[kk, o], g.at[k, o % 2, y, o // 2, place],
                     s_u.at[k], r_s.at[k], dev(dp=y * SUBS + o))

    wait(mix, l_one.at[0])
    s_full = jnp.concatenate([mix[i] for i in range(mix.shape[0])], axis=1)
    s_hi = s_full.astype(BF)
    s_lo = (s_full - s_hi.astype(F32)).astype(BF)
    both = jnp.concatenate([s_hi, s_lo], axis=0)
    sb[...] = both
    sall[d] = both
    for j in range(1, DP):
        send(sb, sall.at[d], s_one.at[0], r_one.at[0], dev(dp=(d + j) % DP))

    @pl.when(apart)
    def _():
        send(a_in.at[rows(m, FB)], ai, s_one.at[1], r_one.at[1], dev(dp=x * SUBS + m, tensor=y))

    @pl.when(same)
    def _():
        pltpu.make_async_copy(a_in.at[rows(m, FB)], ai, r_one.at[1]).start()

    pltpu.make_async_copy(ct, cta.at[sec], r_one.at[2]).start()
    for j in range(1, S):
        send(ct, cta.at[sec], s_one.at[2], r_one.at[2], dev(section=(sec + j) % S))

    def step_s(k):
        block = g.at[k, core, y, zh]
        wait(block, r_s.at[k])
        send(block, block, s_s.at[k], r_z.at[k], dev(dp=(d + 2) % SUBS + y * SUBS))
        for j in range(1, Y):
            send(block, block, s_s.at[k], r_y.at[k], dev(dp=((y + j) % Y) * SUBS + m))

    def step_z(k):
        block = g.at[k, core, y, 1 - zh]
        wait(block, r_z.at[k])
        for j in range(1, Y):
            send(block, block, s_z.at[k], r_y.at[k], dev(dp=((y + j) % Y) * SUBS + m))

    def prepare():
        wait(hid, l_one.at[3])
        wait(a, l_one.at[4])
        down = jnp.dot(hid[...], a[...], preferred_element_type=F32)
        dx[x] = down
        for j in range(1, X):
            send(dx.at[x], dx.at[x], s_one.at[3], r_one.at[3], dev(tensor=(x + j) % X))
        wait(sall.at[pl.ds(0, DP - 1)], r_one.at[0])
        expert = lax.broadcasted_iota(jnp.int32, (2 * ex, R), 0)
        column = lax.broadcasted_iota(jnp.int32, (2 * ex, R), 1)
        expand = jnp.where(lax.rem(expert, ex) == lax.div(column, rank), 1.0, 0.0).astype(BF)

        @pl.loop(0, DP)
        def _(owner):
            turned = sall[owner].astype(F32).T.astype(BF)
            se[owner // SUBS, owner % SUBS] = jnp.dot(turned, expand, preferred_element_type=F32)

        wait(ai, r_one.at[1])
        wait(w, l_one.at[1])
        wait(b, l_one.at[2])

    def half(k, c):
        total = None
        back = None
        for zz in range(2):
            f = zz * 2 + c
            left = g[k, c, :, zz].reshape(Y * OWNERS * T, FB)
            t = jnp.dot(left, w[rows(f, FB), :], preferred_element_type=F32)
            q = dot_nt(left, b[:, cols(f, FB)])
            total = t if total is None else total + t
            back = q if back is None else back + q
        return total, back

    def step_m(k):
        kk = k // parts
        active = mine(k)
        wait(g.at[k, 0, pl.ds(0, Y - 1)], r_y.at[k])
        send(g.at[k, core], g.at[k, core], s_c.at[k], r_c.at[k], dev(dp=d + 1 - 2 * core))
        total, back = half(k, core)
        pacc[...] = total
        bacc[...] = back
        wait(g.at[k, 0], r_c.at[k])
        total, back = half(k, 1 - core)
        back = bacc[...] + back
        bacc[...] = back

        @pl.when(active)
        def _():
            bx[x, kk] = bacc[rows(y * OWNERS + place, T), :]
            for j in range(1, X):
                send(bx.at[x, kk], bx.at[x, kk], s_b.at[kk], r_one.at[5], dev(tensor=(x + j) % X))

        first = (k % parts) * OWNERS
        spread = se[:, pl.ds(first, OWNERS), rows(kk, T), :].reshape(Y * OWNERS * T, R)
        weighted = (back * spread).astype(BF)
        pacc[...] += total + dot_nt(weighted, ai[...])

        @pl.when(same)
        def _():
            pacc[...] += g[k, core, :, zh].reshape(Y * OWNERS * T, FB).astype(F32)

        pb[k] = pacc[...].astype(BF).reshape(Y, OWNERS, T, FB)
        for j in range(1, X):
            r = (x + j) % X
            send(pb.at[k, r], rx.at[k, x], s_x.at[k], r_x.at[k], dev(tensor=r))
        own[k] = pacc[rows(x, OWNERS * T), :]

        @pl.when(jnp.logical_and(active, sec < S - 1))
        def _():
            for c in range(2):
                for zz in range(2):
                    send(g.at[k, c, y, zz, place], out.at[kk, c, zz], s_o.at[kk], r_one.at[4], dev(section=sec + 1))

    def step_x(k):
        kk = k // parts
        wait(rx.at[k, pl.ds(0, X - 1)], r_x.at[k])
        total = own[k]
        for j in range(1, X):
            total = total + rx[k, (x + j) % X].reshape(OWNERS * T, FB).astype(F32)
        sp[k] = total.astype(BF).reshape(OWNERS, T, FB)

        @pl.when(sec > 0)
        def _():
            send(sp.at[k], g.at[k, core, x, zh], s_p.at[k], r_s.at[k],
                 dev(dp=x * SUBS + m, section=sec - 1, tensor=y))

        @pl.when(bottom)
        def _():
            for o in range(OWNERS):
                owner = (k % parts) * OWNERS + o
                here = jnp.logical_and(same, m == owner)

                @pl.when(here)
                def _():
                    pltpu.make_async_copy(sp.at[k, o], out.at[kk, core, zh], r_one.at[4]).start()

                @pl.when(jnp.logical_not(here))
                def _():
                    send(sp.at[k, o], out.at[kk, core, zh], s_p.at[k], r_one.at[4],
                         dev(dp=x * SUBS + owner, tensor=y))

    NK = N // parts
    tokens = NK * T
    FD = hl.shape[2]

    def scalings():
        wait(bx.at[pl.ds(0, X - 1)], r_one.at[5])
        wait(dx.at[pl.ds(0, X - 1)], r_one.at[3])
        back = bx[0].reshape(tokens, R)
        down = dx[0]
        for j in range(1, X):
            back = back + bx[j].reshape(tokens, R)
            down = down + dx[j]
        product = down * back
        expert = lax.broadcasted_iota(jnp.int32, (ex, R), 0)
        column = lax.broadcasted_iota(jnp.int32, (ex, R), 1)
        group = jnp.where(expert == lax.div(column, rank), 1.0, 0.0).astype(F32)
        turned = dot_nt(group, product, lax.Precision.HIGHEST)
        sga[sec] = turned
        for j in range(1, S):
            send(sga.at[sec], sga.at[sec], s_one.at[5], r_one.at[6], dev(section=(sec + j) % S))
        per = tokens // mix.shape[0]
        for i in range(mix.shape[0]):
            scale[i] = turned[:, i * per:(i + 1) * per]

        wait(states, l_one.at[5])
        t_hi = turned.astype(BF)
        t_lo = (turned - t_hi.astype(F32)).astype(BF)
        sums = (jnp.dot(t_hi, states[...], preferred_element_type=F32)
                + jnp.dot(t_lo, states[...], preferred_element_type=F32))
        for e in range(DP):
            hl[e] = sums[:, e * FD:(e + 1) * FD]
        for j in range(1, DP):
            e = (d + j) % DP
            send(hl.at[e], hx.at[d], s_one.at[6], r_one.at[7], dev(dp=e))
        hx[d] = hl[d]

    steps = {"S": step_s, "Z": step_z, "M": step_m, "X": step_x}
    behind = dict(ORDER)

    turns = N + max(behind.values())

    @pl.loop(0, turns + 1)
    def _(i):
        @pl.when(i == jnp.where(top, behind["M"], 0))
        def _():
            prepare()

        @pl.when(i == jnp.where(bottom, N + behind["M"], turns))
        def _():
            scalings()

        for name, lag in ORDER:
            @pl.when(jnp.logical_and(i >= lag, i < N + lag))
            def _():
                steps[name](i - lag)

    wait(hx.at[pl.ds(0, DP - 1)], r_one.at[7])
    total = hx[0]
    for j in range(1, DP):
        total = total + hx[j]
    total = total * (1.0 / math.sqrt(tokens * DP))
    hg[d] = total
    for j in range(1, DP):
        send(hg.at[d], hg.at[d], s_one.at[7], r_one.at[8], dev(dp=(d + j) % DP))

    wait(cta, r_one.at[2])
    wait(sga.at[pl.ds(0, S - 1)], r_one.at[6])
    left = sga[...].reshape(S * ex, tokens).T
    right = cta[...].reshape(S * ex, -1)
    hidden[...] = jnp.dot(left, right, precision=lax.Precision.HIGHEST, preferred_element_type=F32)

    wait(hx.at[pl.ds(0, DP - 1)], r_one.at[8])
    for e in range(DP):
        head[:, e * FD:(e + 1) * FD] = hg[e]
    wait(out, r_one.at[4])
    wait(sall.at[pl.ds(0, DP - 1)], s_one.at[0])

    @pl.when(apart)
    def _():
        wait(ai, s_one.at[1])

    wait(cta.at[pl.ds(0, S - 1)], s_one.at[2])
    wait(dx.at[pl.ds(0, X - 1)], s_one.at[3])
    wait(sga.at[pl.ds(0, S - 1)], s_one.at[5])
    wait(hx.at[pl.ds(0, DP - 1)], s_one.at[6])
    wait(hx.at[pl.ds(0, DP - 1)], s_one.at[7])

    @pl.loop(0, N)
    def _(k):
        kk = k // parts
        wait(g.at[k, 0, :, 0], s_s.at[k])
        wait(g.at[k, 0, pl.ds(0, Y - 1), 0], s_z.at[k])
        wait(g.at[k, 0], s_c.at[k])
        wait(rx.at[k, pl.ds(0, X - 1)], s_x.at[k])
        active = mine(k)

        @pl.when(active)
        def _():
            wait(bx.at[pl.ds(0, X - 1), kk], s_b.at[kk])

            @pl.when(top)
            def _():
                wait(out.at[kk, 0, pl.ds(0, 1)], s_u.at[k])
                wait(out.at[kk, 1], s_u.at[k])

            @pl.when(sec < S - 1)
            def _():
                wait(out.at[kk], s_o.at[kk])

        local = jnp.logical_and(jnp.logical_and(bottom, same), active)

        @pl.when(local)
        def _():
            if OWNERS > 1:
                wait(sp.at[k, pl.ds(0, OWNERS - 1)], s_p.at[k])

        @pl.when(jnp.logical_not(local))
        def _():
            wait(sp.at[k], s_p.at[k])


def on_device(u, saved, w, a, b, mix, states, classifier):
    X, S, DP = (lax.axis_size(n) for n in ("tensor", "section", "dp"))
    Y = DP // SUBS
    micro, per, F = u.shape
    T = TOK
    tokens = micro * per
    NK = tokens // T
    N = NK * (SUBS // OWNERS)
    FB = w.shape[2]
    R = a.shape[2]
    ex = mix.shape[2]
    vmem = pl.BlockSpec(memory_space=pltpu.VMEM)
    far = pl.BlockSpec(memory_space=pltpu.HBM)
    dma = pltpu.SemaphoreType.DMA
    sizes = (X, Y, S, DP, N, R)
    out, scale, head, hidden = pl.pallas_call(
        functools.partial(kernel, sizes),
        out_shape=(
            jax.ShapeDtypeStruct((NK, 2, 2, T, FB), BF),
            jax.ShapeDtypeStruct((micro, ex, per), F32),
            jax.ShapeDtypeStruct((ex, F), F32),
            jax.ShapeDtypeStruct((tokens, F), F32),
        ),
        in_specs=[far] * 8,
        out_specs=(vmem,) * 4,
        scratch_shapes=[
            pltpu.VMEM((NK, T, F), BF),
            pltpu.VMEM((NK, SUBS, T, FB), BF),
            pltpu.VMEM((tokens, F), BF),
            pltpu.VMEM((F, FB), BF),
            pltpu.VMEM((F, R), BF),
            pltpu.VMEM((R, F), BF),
            pltpu.VMEM((micro, ex, per), F32),
            pltpu.VMEM((tokens, F), BF),
            pltpu.VMEM((N, 2, Y, 2, OWNERS, T, FB), BF),
            pltpu.VMEM((N, Y, OWNERS, T, FB), BF),
            pltpu.VMEM((N, X, OWNERS, T, FB), BF),
            pltpu.VMEM((N, OWNERS * T, FB), F32),
            pltpu.VMEM((N, OWNERS, T, FB), BF),
            pltpu.VMEM((Y, SUBS, tokens, R), F32),
            pltpu.VMEM((2 * ex, tokens), BF),
            pltpu.VMEM((DP, 2 * ex, tokens), BF),
            pltpu.VMEM((FB, R), BF),
            pltpu.VMEM((X, tokens, R), F32),
            pltpu.VMEM((X, NK, T, R), F32),
            pltpu.VMEM((Y * OWNERS * T, FB), F32),
            pltpu.VMEM((Y * OWNERS * T, R), F32),
            pltpu.VMEM((S, ex, F), F32),
            pltpu.VMEM((S, ex, tokens), F32),
            pltpu.VMEM((DP, ex, F // DP), F32),
            pltpu.VMEM((DP, ex, F // DP), F32),
            pltpu.VMEM((DP, ex, F // DP), F32),
        ] + [dma((N,))] * 13 + [dma((9,)), dma((8,)), dma((7,))],
        compiler_params=pltpu.CompilerParams(
            collective_id=0, has_side_effects=True, vmem_limit_bytes=60 * 1024 * 1024,
        ),
    )(
        u.reshape(NK, T, F),
        saved.reshape(tokens, F),
        w[0], a[0], b[0],
        mix.transpose(0, 2, 1),
        states.reshape(tokens, F),
        classifier.T,
    )
    grads = out.reshape(micro, per // T, 2, 2, T, FB).transpose(0, 1, 4, 3, 2, 5).reshape(1, micro, per, F)
    return grads, scale.transpose(0, 2, 1), head.T, hidden.reshape(micro, per, F)


def solution(mesh):
    return jax.shard_map(
        on_device,
        mesh=mesh,
        in_specs=(
            P(None, "dp", "tensor"),
            P("section", None, "dp", "tensor"),
            P("section", "tensor", "dp"),
            P("section", "tensor", None),
            P("section", None, "tensor"),
            P(None, "dp", "section"),
            P(None, "dp", "tensor"),
            P("tensor", "section"),
        ),
        out_specs=(
            P("section", None, "dp", "tensor"),
            P(None, "dp", "section"),
            P("tensor", "section"),
            P(None, "dp", "tensor"),
        ),
        check_vma=False,
    )
```

```python
import functools
import math

import jax
import jax.numpy as jnp
from jax import lax
from jax.experimental import pallas as pl
from jax.experimental.pallas import tpu as pltpu
from jax.sharding import PartitionSpec as P

BF = jnp.bfloat16
F32 = jnp.float32
NT_DIMS = (((1,), (1,)), ((), ()))
SUBS = 4
TOK = 16
OWNERS = 2
ORDER = (("S", 0), ("M", 3), ("R", 1), ("Z", 1), ("X", 4))


def dot_nt(a, b, precision=None):
    return lax.dot_general(a, b, NT_DIMS, precision=precision, preferred_element_type=F32)


def kernel(
    sizes,
    u, hid_in, w_in, a_in, b_in, mix_in, states_in, ct,
    grads, scale, head, hidden,
    out, uv, us, hid, w, a, b, mix, states,
    g, pb, rx, own, sp, se, sb, sall, ai, dx, bx, pacc, bacc, cta, sga, hl, hx, hg,
    r_s, r_z, r_y, r_c, r_x, r_p, r_n,
    s_s, s_z, s_c, s_x, s_p, s_o, s_b, s_u, s_r,
    r_one, s_one, l_one,
):
    X, Y, S, DP, N, R = sizes
    T = TOK
    FB = w.shape[1]
    ex = mix.shape[1]
    rank = R // ex
    parts = SUBS // OWNERS
    d = lax.axis_index("dp")
    sec = lax.axis_index("section")
    x = lax.axis_index("tensor")
    y = d // SUBS
    m = d % SUBS
    zh = m // 2
    core = m % 2
    place = m % OWNERS

    def dev(dp=None, section=None, tensor=None):
        return {
            "dp": d if dp is None else dp,
            "section": sec if section is None else section,
            "tensor": x if tensor is None else tensor,
        }

    def send(src, dst, ssem, rsem, target):
        pltpu.make_async_remote_copy(
            src_ref=src, dst_ref=dst, send_sem=ssem, recv_sem=rsem,
            device_id=target, device_id_type=pl.DeviceIdType.MESH,
        ).start()

    def wait(ref, sem):
        pltpu.make_async_copy(ref, ref, sem).wait()

    def cols(index, width):
        return pl.ds(pl.multiple_of(index * width, 128), width)

    def rows(index, height):
        return pl.ds(pl.multiple_of(index * height, 16), height)

    def mine(k):
        return m // OWNERS == k % parts

    same = x == y
    apart = jnp.logical_not(same)
    top = sec == S - 1
    bottom = sec == 0

    @pl.when(top)
    def _():
        pltpu.make_async_copy(u, uv, l_one.at[6]).start()

    loads = ((mix_in, mix), (w_in, w), (b_in, b), (hid_in, hid), (a_in, a), (states_in, states))
    for i, (far, near) in enumerate(loads):
        pltpu.make_async_copy(far, near, l_one.at[i]).start()

    barrier = pltpu.get_barrier_semaphore()

    def hello(target):
        pl.semaphore_signal(barrier, inc=1, device_id=target, device_id_type=pl.DeviceIdType.MESH)

    for j in range(1, DP):
        hello(dev(dp=(d + j) % DP))
    for j in range(1, X):
        hello(dev(tensor=(x + j) % X))
    for j in range(1, S):
        hello(dev(section=(sec + j) % S))

    @pl.when(apart)
    def _():
        for o in range(SUBS):
            hello(dev(dp=x * SUBS + o, tensor=y))

        @pl.when(sec > 0)
        def _():
            hello(dev(dp=x * SUBS + m, section=sec - 1, tensor=y))

        @pl.when(sec < S - 1)
        def _():
            hello(dev(dp=x * SUBS + m, section=sec + 1, tensor=y))

    extra = SUBS + jnp.where(bottom, 0, 1) + jnp.where(top, 0, 1)
    pl.semaphore_wait(barrier, DP - 1 + X - 1 + S - 1 + jnp.where(same, 0, extra))

    @pl.when(top)
    def _():
        wait(uv, l_one.at[6])

        @pl.loop(0, N // parts)
        def _(kk):
            k = kk * parts + m // OWNERS
            for o in range(SUBS):
                us[kk, o] = uv[kk, :, o * FB:(o + 1) * FB]
            pltpu.make_async_copy(us.at[kk, m], g.at[k, core, y, zh, place], r_s.at[k]).start()
            for j in range(1, SUBS):
                o = (m + j) % SUBS
                send(us.at[kk, o], g.at[k, o % 2, y, o // 2, place],
                     s_u.at[k], r_s.at[k], dev(dp=y * SUBS + o))

    wait(mix, l_one.at[0])
    s_full = jnp.concatenate([mix[i] for i in range(mix.shape[0])], axis=1)
    s_hi = s_full.astype(BF)
    s_lo = (s_full - s_hi.astype(F32)).astype(BF)
    both = jnp.concatenate([s_hi, s_lo], axis=0)
    sb[...] = both
    sall[d] = both
    for j in range(1, DP):
        send(sb, sall.at[d], s_one.at[0], r_one.at[0], dev(dp=(d + j) % DP))

    @pl.when(apart)
    def _():
        send(a_in.at[rows(m, FB)], ai, s_one.at[1], r_one.at[1], dev(dp=x * SUBS + m, tensor=y))

    @pl.when(same)
    def _():
        pltpu.make_async_copy(a_in.at[rows(m, FB)], ai, r_one.at[1]).start()

    pltpu.make_async_copy(ct, cta.at[sec], r_one.at[2]).start()
    for j in range(1, S):
        send(ct, cta.at[sec], s_one.at[2], r_one.at[2], dev(section=(sec + j) % S))

    def step_s(k):
        block = g.at[k, core, y, zh]
        wait(block, r_s.at[k])
        send(block, block, s_s.at[k], r_z.at[k], dev(dp=(d + 2) % SUBS + y * SUBS))
        send(block, block, s_s.at[k], r_p.at[k], dev(dp=((y + 1) % Y) * SUBS + m))
        send(block, block, s_s.at[k], r_n.at[k], dev(dp=((y + Y - 1) % Y) * SUBS + m))

    def step_r(k):
        before = (y + Y - 1) % Y
        after = (y + 1) % Y
        half = OWNERS // 2
        wait(g.at[k, core, before, zh], r_p.at[k])
        lower = g.at[k, core, before, zh, pl.ds(0, half)]
        send(lower, lower, s_r.at[k], r_y.at[k], dev(dp=after * SUBS + m))
        wait(g.at[k, core, after, zh], r_n.at[k])
        upper = g.at[k, core, after, zh, pl.ds(half, half)]
        send(upper, upper, s_r.at[k], r_y.at[k], dev(dp=before * SUBS + m))

    def step_z(k):
        block = g.at[k, core, y, 1 - zh]
        wait(block, r_z.at[k])
        for j in range(1, Y):
            send(block, block, s_z.at[k], r_y.at[k], dev(dp=((y + j) % Y) * SUBS + m))

    def prepare():
        wait(hid, l_one.at[3])
        wait(a, l_one.at[4])
        down = jnp.dot(hid[...], a[...], preferred_element_type=F32)
        dx[x] = down
        for j in range(1, X):
            send(dx.at[x], dx.at[x], s_one.at[3], r_one.at[3], dev(tensor=(x + j) % X))
        wait(sall.at[pl.ds(0, DP - 1)], r_one.at[0])
        expert = lax.broadcasted_iota(jnp.int32, (2 * ex, R), 0)
        column = lax.broadcasted_iota(jnp.int32, (2 * ex, R), 1)
        expand = jnp.where(lax.rem(expert, ex) == lax.div(column, rank), 1.0, 0.0).astype(BF)

        @pl.loop(0, DP)
        def _(owner):
            turned = sall[owner].astype(F32).T.astype(BF)
            se[owner // SUBS, owner % SUBS] = jnp.dot(turned, expand, preferred_element_type=F32)

        wait(ai, r_one.at[1])
        wait(w, l_one.at[1])
        wait(b, l_one.at[2])

    def half(k, c):
        total = None
        back = None
        for zz in range(2):
            f = zz * 2 + c
            left = g[k, c, :, zz].reshape(Y * OWNERS * T, FB)
            t = jnp.dot(left, w[rows(f, FB), :], preferred_element_type=F32)
            q = dot_nt(left, b[:, cols(f, FB)])
            total = t if total is None else total + t
            back = q if back is None else back + q
        return total, back

    def step_m(k):
        kk = k // parts
        active = mine(k)
        wait(g.at[k, 0, pl.ds(0, 2)], r_y.at[k])
        send(g.at[k, core], g.at[k, core], s_c.at[k], r_c.at[k], dev(dp=d + 1 - 2 * core))
        total, back = half(k, core)
        pacc[...] = total
        bacc[...] = back
        wait(g.at[k, 0], r_c.at[k])
        total, back = half(k, 1 - core)
        back = bacc[...] + back
        bacc[...] = back

        @pl.when(active)
        def _():
            bx[x, kk] = bacc[rows(y * OWNERS + place, T), :]
            for j in range(1, X):
                send(bx.at[x, kk], bx.at[x, kk], s_b.at[kk], r_one.at[5], dev(tensor=(x + j) % X))

        first = (k % parts) * OWNERS
        spread = se[:, pl.ds(first, OWNERS), rows(kk, T), :].reshape(Y * OWNERS * T, R)
        weighted = (back * spread).astype(BF)
        pacc[...] += total + dot_nt(weighted, ai[...])

        @pl.when(same)
        def _():
            pacc[...] += g[k, core, :, zh].reshape(Y * OWNERS * T, FB).astype(F32)

        pb[k] = pacc[...].astype(BF).reshape(Y, OWNERS, T, FB)
        for j in range(1, X):
            r = (x + j) % X
            send(pb.at[k, r], rx.at[k, x], s_x.at[k], r_x.at[k], dev(tensor=r))
        own[k] = pacc[rows(x, OWNERS * T), :]

        @pl.when(jnp.logical_and(active, sec < S - 1))
        def _():
            for c in range(2):
                for zz in range(2):
                    send(g.at[k, c, y, zz, place], out.at[kk, c, zz], s_o.at[kk], r_one.at[4], dev(section=sec + 1))

    def step_x(k):
        kk = k // parts
        wait(rx.at[k, pl.ds(0, X - 1)], r_x.at[k])
        total = own[k]
        for j in range(1, X):
            total = total + rx[k, (x + j) % X].reshape(OWNERS * T, FB).astype(F32)
        sp[k] = total.astype(BF).reshape(OWNERS, T, FB)

        @pl.when(sec > 0)
        def _():
            send(sp.at[k], g.at[k, core, x, zh], s_p.at[k], r_s.at[k],
                 dev(dp=x * SUBS + m, section=sec - 1, tensor=y))

        @pl.when(bottom)
        def _():
            for o in range(OWNERS):
                owner = (k % parts) * OWNERS + o
                here = jnp.logical_and(same, m == owner)

                @pl.when(here)
                def _():
                    pltpu.make_async_copy(sp.at[k, o], out.at[kk, core, zh], r_one.at[4]).start()

                @pl.when(jnp.logical_not(here))
                def _():
                    send(sp.at[k, o], out.at[kk, core, zh], s_p.at[k], r_one.at[4],
                         dev(dp=x * SUBS + owner, tensor=y))

    NK = N // parts
    tokens = NK * T
    FD = hl.shape[2]

    def scalings():
        wait(bx.at[pl.ds(0, X - 1)], r_one.at[5])
        wait(dx.at[pl.ds(0, X - 1)], r_one.at[3])
        back = bx[0].reshape(tokens, R)
        down = dx[0]
        for j in range(1, X):
            back = back + bx[j].reshape(tokens, R)
            down = down + dx[j]
        product = down * back
        expert = lax.broadcasted_iota(jnp.int32, (ex, R), 0)
        column = lax.broadcasted_iota(jnp.int32, (ex, R), 1)
        group = jnp.where(expert == lax.div(column, rank), 1.0, 0.0).astype(F32)
        turned = dot_nt(group, product, lax.Precision.HIGHEST)
        sga[sec] = turned
        for j in range(1, S):
            send(sga.at[sec], sga.at[sec], s_one.at[5], r_one.at[6], dev(section=(sec + j) % S))
        per = tokens // mix.shape[0]
        for i in range(mix.shape[0]):
            scale[i] = turned[:, i * per:(i + 1) * per]

        wait(states, l_one.at[5])
        t_hi = turned.astype(BF)
        t_lo = (turned - t_hi.astype(F32)).astype(BF)
        sums = (jnp.dot(t_hi, states[...], preferred_element_type=F32)
                + jnp.dot(t_lo, states[...], preferred_element_type=F32))
        for e in range(DP):
            hl[e] = sums[:, e * FD:(e + 1) * FD].astype(BF)
        for j in range(1, DP):
            e = (d + j) % DP
            send(hl.at[e], hx.at[d], s_one.at[6], r_one.at[7], dev(dp=e))
        hx[d] = hl[d]

    steps = {"S": step_s, "Z": step_z, "R": step_r, "M": step_m, "X": step_x}
    behind = dict(ORDER)

    turns = N + max(behind.values())

    @pl.loop(0, turns + 1)
    def _(i):
        @pl.when(i == jnp.where(top, behind["M"], 0))
        def _():
            prepare()

        @pl.when(i == jnp.where(bottom, N + behind["M"], turns))
        def _():
            scalings()

        for name, lag in ORDER:
            @pl.when(jnp.logical_and(i >= lag, i < N + lag))
            def _():
                steps[name](i - lag)

    wait(hx.at[pl.ds(0, DP - 1)], r_one.at[7])
    total = hx[0].astype(F32)
    for j in range(1, DP):
        total = total + hx[j].astype(F32)
    hg[d] = (total * (1.0 / math.sqrt(tokens * DP))).astype(BF)
    for j in range(1, DP):
        send(hg.at[d], hg.at[d], s_one.at[7], r_one.at[8], dev(dp=(d + j) % DP))

    wait(cta, r_one.at[2])
    wait(sga.at[pl.ds(0, S - 1)], r_one.at[6])
    left = sga[...].reshape(S * ex, tokens).T
    right = cta[...].reshape(S * ex, -1)
    hidden[...] = jnp.dot(left, right, precision=lax.Precision.HIGHEST, preferred_element_type=F32)

    wait(hx.at[pl.ds(0, DP - 1)], r_one.at[8])
    for e in range(DP):
        head[:, e * FD:(e + 1) * FD] = hg[e].astype(F32)
    wait(out, r_one.at[4])
    for f in range(SUBS):
        grads[:, :, f * FB:(f + 1) * FB] = out[:, f % 2, f // 2]
    wait(sall.at[pl.ds(0, DP - 1)], s_one.at[0])

    @pl.when(apart)
    def _():
        wait(ai, s_one.at[1])

    wait(cta.at[pl.ds(0, S - 1)], s_one.at[2])
    wait(dx.at[pl.ds(0, X - 1)], s_one.at[3])
    wait(sga.at[pl.ds(0, S - 1)], s_one.at[5])
    wait(hx.at[pl.ds(0, DP - 1)], s_one.at[6])
    wait(hx.at[pl.ds(0, DP - 1)], s_one.at[7])

    @pl.loop(0, N)
    def _(k):
        kk = k // parts
        wait(g.at[k, 0, pl.ds(0, Y - 1), 0], s_s.at[k])
        wait(g.at[k, 0, 0, 0], s_r.at[k])
        wait(g.at[k, 0, pl.ds(0, Y - 1), 0], s_z.at[k])
        wait(g.at[k, 0], s_c.at[k])
        wait(rx.at[k, pl.ds(0, X - 1)], s_x.at[k])
        active = mine(k)

        @pl.when(active)
        def _():
            wait(bx.at[pl.ds(0, X - 1), kk], s_b.at[kk])

            @pl.when(top)
            def _():
                wait(out.at[kk, 0, pl.ds(0, 1)], s_u.at[k])
                wait(out.at[kk, 1], s_u.at[k])

            @pl.when(sec < S - 1)
            def _():
                wait(out.at[kk], s_o.at[kk])

        local = jnp.logical_and(jnp.logical_and(bottom, same), active)

        @pl.when(local)
        def _():
            if OWNERS > 1:
                wait(sp.at[k, pl.ds(0, OWNERS - 1)], s_p.at[k])

        @pl.when(jnp.logical_not(local))
        def _():
            wait(sp.at[k], s_p.at[k])


def finish(*refs):
    copies = [pltpu.make_async_copy(refs[i], refs[4 + i], refs[8].at[i]) for i in range(4)]
    for copy in copies:
        copy.start()
    for copy in copies:
        copy.wait()


def on_device(u, saved, w, a, b, mix, states, classifier):
    X, S, DP = (lax.axis_size(n) for n in ("tensor", "section", "dp"))
    Y = DP // SUBS
    micro, per, F = u.shape
    T = TOK
    tokens = micro * per
    NK = tokens // T
    N = NK * (SUBS // OWNERS)
    FB = w.shape[2]
    R = a.shape[2]
    ex = mix.shape[2]
    vmem = pl.BlockSpec(memory_space=pltpu.VMEM)
    far = pl.BlockSpec(memory_space=pltpu.HBM)
    dma = pltpu.SemaphoreType.DMA
    sizes = (X, Y, S, DP, N, R)
    shapes = (
        jax.ShapeDtypeStruct((NK, T, F), BF),
        jax.ShapeDtypeStruct((micro, ex, per), F32),
        jax.ShapeDtypeStruct((ex, F), F32),
        jax.ShapeDtypeStruct((tokens, F), F32),
    )
    results = pl.pallas_call(
        functools.partial(kernel, sizes),
        out_shape=shapes,
        in_specs=[far] * 8,
        out_specs=(vmem,) * 4,
        scratch_shapes=[
            pltpu.VMEM((NK, 2, 2, T, FB), BF),
            pltpu.VMEM((NK, T, F), BF),
            pltpu.VMEM((NK, SUBS, T, FB), BF),
            pltpu.VMEM((tokens, F), BF),
            pltpu.VMEM((F, FB), BF),
            pltpu.VMEM((F, R), BF),
            pltpu.VMEM((R, F), BF),
            pltpu.VMEM((micro, ex, per), F32),
            pltpu.VMEM((tokens, F), BF),
            pltpu.VMEM((N, 2, Y, 2, OWNERS, T, FB), BF),
            pltpu.VMEM((N, Y, OWNERS, T, FB), BF),
            pltpu.VMEM((N, X, OWNERS, T, FB), BF),
            pltpu.VMEM((N, OWNERS * T, FB), F32),
            pltpu.VMEM((N, OWNERS, T, FB), BF),
            pltpu.VMEM((Y, SUBS, tokens, R), F32),
            pltpu.VMEM((2 * ex, tokens), BF),
            pltpu.VMEM((DP, 2 * ex, tokens), BF),
            pltpu.VMEM((FB, R), BF),
            pltpu.VMEM((X, tokens, R), F32),
            pltpu.VMEM((X, NK, T, R), F32),
            pltpu.VMEM((Y * OWNERS * T, FB), F32),
            pltpu.VMEM((Y * OWNERS * T, R), F32),
            pltpu.VMEM((S, ex, F), F32),
            pltpu.VMEM((S, ex, tokens), F32),
            pltpu.VMEM((DP, ex, F // DP), BF),
            pltpu.VMEM((DP, ex, F // DP), BF),
            pltpu.VMEM((DP, ex, F // DP), BF),
        ] + [dma((N,))] * 16 + [dma((9,)), dma((8,)), dma((7,))],
        compiler_params=pltpu.CompilerParams(
            collective_id=0, has_side_effects=True, vmem_limit_bytes=60 * 1024 * 1024,
        ),
    )(
        u.reshape(NK, T, F),
        saved.reshape(tokens, F),
        w[0], a[0], b[0],
        mix.transpose(0, 2, 1),
        states.reshape(tokens, F),
        classifier.T,
    )
    grads, scale, head, hidden = pl.pallas_call(
        finish,
        out_shape=shapes,
        in_specs=[vmem] * 4,
        out_specs=(far,) * 4,
        scratch_shapes=[dma((4,))],
    )(*results)
    grads = grads.reshape(1, micro, per, F)
    return grads, scale.transpose(0, 2, 1), head.T, hidden.reshape(micro, per, F)


def solution(mesh):
    return jax.shard_map(
        on_device,
        mesh=mesh,
        in_specs=(
            P(None, "dp", "tensor"),
            P("section", None, "dp", "tensor"),
            P("section", "tensor", "dp"),
            P("section", "tensor", None),
            P("section", None, "tensor"),
            P(None, "dp", "section"),
            P(None, "dp", "tensor"),
            P("tensor", "section"),
        ),
        out_specs=(
            P("section", None, "dp", "tensor"),
            P(None, "dp", "section"),
            P("tensor", "section"),
            P(None, "dp", "tensor"),
        ),
        check_vma=False,
    )
```

```python
import functools
import math

import jax
import jax.numpy as jnp
from jax import lax
from jax.experimental import pallas as pl
from jax.experimental.pallas import tpu as pltpu
from jax.sharding import PartitionSpec as P

BF = jnp.bfloat16
F32 = jnp.float32
NT_DIMS = (((1,), (1,)), ((), ()))
SUBS = 4
TOK = 16
OWNERS = 2
ORDER = (("S", 0), ("M", 3), ("R", 1), ("Z", 1), ("X", 4))


def dot_nt(a, b, precision=None):
    return lax.dot_general(a, b, NT_DIMS, precision=precision, preferred_element_type=F32)


def kernel(
    sizes,
    u, hid_in, w_in, a_in, b_in, mix_in, states_in, ct,
    grads, scale, head, hidden,
    out, uv, us, hid, w, a, b, mix, states,
    g, pb, rx, own, sp, se, sb, sall, ai, dx, bx, pacc, bacc, cta, sga, hl, hx, hg,
    r_s, r_z, r_y, r_c, r_x, r_p, r_n,
    s_s, s_z, s_c, s_x, s_p, s_o, s_b, s_u, s_r,
    r_one, s_one, l_one,
):
    X, Y, S, DP, N, R = sizes
    T = TOK
    FB = w.shape[1]
    ex = mix.shape[1]
    rank = R // ex
    parts = SUBS // OWNERS
    d = lax.axis_index("dp")
    sec = lax.axis_index("section")
    x = lax.axis_index("tensor")
    y = d // SUBS
    m = d % SUBS
    zh = m // 2
    core = m % 2
    place = m % OWNERS

    def dev(dp=None, section=None, tensor=None):
        return {
            "dp": d if dp is None else dp,
            "section": sec if section is None else section,
            "tensor": x if tensor is None else tensor,
        }

    def send(src, dst, ssem, rsem, target):
        pltpu.make_async_remote_copy(
            src_ref=src, dst_ref=dst, send_sem=ssem, recv_sem=rsem,
            device_id=target, device_id_type=pl.DeviceIdType.MESH,
        ).start()

    def wait(ref, sem):
        pltpu.make_async_copy(ref, ref, sem).wait()

    def cols(index, width):
        return pl.ds(pl.multiple_of(index * width, 128), width)

    def rows(index, height):
        return pl.ds(pl.multiple_of(index * height, 16), height)

    def mine(k):
        return m // OWNERS == k % parts

    same = x == y
    apart = jnp.logical_not(same)
    top = sec == S - 1
    bottom = sec == 0

    @pl.when(top)
    def _():
        pltpu.make_async_copy(u, uv, l_one.at[6]).start()

    loads = ((mix_in, mix), (w_in, w), (b_in, b), (hid_in, hid), (a_in, a), (states_in, states))
    for i, (far, near) in enumerate(loads):
        pltpu.make_async_copy(far, near, l_one.at[i]).start()

    barrier = pltpu.get_barrier_semaphore()

    def hello(target):
        pl.semaphore_signal(barrier, inc=1, device_id=target, device_id_type=pl.DeviceIdType.MESH)

    for j in range(1, DP):
        hello(dev(dp=(d + j) % DP))
    for j in range(1, X):
        hello(dev(tensor=(x + j) % X))
    for j in range(1, S):
        hello(dev(section=(sec + j) % S))

    @pl.when(apart)
    def _():
        for o in range(SUBS):
            hello(dev(dp=x * SUBS + o, tensor=y))

        @pl.when(sec > 0)
        def _():
            hello(dev(dp=x * SUBS + m, section=sec - 1, tensor=y))

        @pl.when(sec < S - 1)
        def _():
            hello(dev(dp=x * SUBS + m, section=sec + 1, tensor=y))

    extra = SUBS + jnp.where(bottom, 0, 1) + jnp.where(top, 0, 1)
    pl.semaphore_wait(barrier, DP - 1 + X - 1 + S - 1 + jnp.where(same, 0, extra))

    @pl.when(top)
    def _():
        wait(uv, l_one.at[6])

        @pl.loop(0, N // parts)
        def _(kk):
            k = kk * parts + m // OWNERS
            for o in range(SUBS):
                us[kk, o] = uv[kk, :, o * FB:(o + 1) * FB]
            pltpu.make_async_copy(us.at[kk, m], g.at[k, core, y, zh, place], r_s.at[k]).start()
            for j in range(1, SUBS):
                o = (m + j) % SUBS
                send(us.at[kk, o], g.at[k, o % 2, y, o // 2, place],
                     s_u.at[k], r_s.at[k], dev(dp=y * SUBS + o))

    wait(mix, l_one.at[0])
    s_full = jnp.concatenate([mix[i] for i in range(mix.shape[0])], axis=1)
    s_hi = s_full.astype(BF)
    s_lo = (s_full - s_hi.astype(F32)).astype(BF)
    both = jnp.concatenate([s_hi, s_lo], axis=0)
    sb[...] = both
    sall[d] = both
    for j in range(1, DP):
        send(sb, sall.at[d], s_one.at[0], r_one.at[0], dev(dp=(d + j) % DP))

    @pl.when(apart)
    def _():
        send(a_in.at[rows(m, FB)], ai, s_one.at[1], r_one.at[1], dev(dp=x * SUBS + m, tensor=y))

    @pl.when(same)
    def _():
        pltpu.make_async_copy(a_in.at[rows(m, FB)], ai, r_one.at[1]).start()

    pltpu.make_async_copy(ct, cta.at[sec], r_one.at[2]).start()
    for j in range(1, S):
        send(ct, cta.at[sec], s_one.at[2], r_one.at[2], dev(section=(sec + j) % S))

    def step_s(k):
        block = g.at[k, core, y, zh]
        wait(block, r_s.at[k])
        send(block, block, s_s.at[k], r_z.at[k], dev(dp=(d + 2) % SUBS + y * SUBS))
        send(block, block, s_s.at[k], r_p.at[k], dev(dp=((y + 1) % Y) * SUBS + m))
        send(block, block, s_s.at[k], r_n.at[k], dev(dp=((y + Y - 1) % Y) * SUBS + m))

    def step_r(k):
        before = (y + Y - 1) % Y
        after = (y + 1) % Y
        half = OWNERS // 2
        wait(g.at[k, core, before, zh], r_p.at[k])
        lower = g.at[k, core, before, zh, pl.ds(0, half)]
        send(lower, lower, s_r.at[k], r_y.at[k], dev(dp=after * SUBS + m))
        wait(g.at[k, core, after, zh], r_n.at[k])
        upper = g.at[k, core, after, zh, pl.ds(half, half)]
        send(upper, upper, s_r.at[k], r_y.at[k], dev(dp=before * SUBS + m))

    def step_z(k):
        block = g.at[k, core, y, 1 - zh]
        wait(block, r_z.at[k])
        for j in (2, 1, 3):
            send(block, block, s_z.at[k], r_y.at[k], dev(dp=((y + j) % Y) * SUBS + m))

    def prepare():
        wait(hid, l_one.at[3])
        wait(a, l_one.at[4])
        down = jnp.dot(hid[...], a[...], preferred_element_type=F32)
        dx[x] = down
        for j in range(1, X):
            send(dx.at[x], dx.at[x], s_one.at[3], r_one.at[3], dev(tensor=(x + j) % X))
        wait(sall.at[pl.ds(0, DP - 1)], r_one.at[0])
        expert = lax.broadcasted_iota(jnp.int32, (2 * ex, R), 0)
        column = lax.broadcasted_iota(jnp.int32, (2 * ex, R), 1)
        expand = jnp.where(lax.rem(expert, ex) == lax.div(column, rank), 1.0, 0.0).astype(BF)

        @pl.loop(0, DP)
        def _(owner):
            turned = sall[owner].astype(F32).T.astype(BF)
            se[owner // SUBS, owner % SUBS] = jnp.dot(turned, expand, preferred_element_type=F32)

        wait(ai, r_one.at[1])
        wait(w, l_one.at[1])
        wait(b, l_one.at[2])

    def half(k, c):
        total = None
        back = None
        for zz in range(2):
            f = zz * 2 + c
            left = g[k, c, :, zz].reshape(Y * OWNERS * T, FB)
            t = jnp.dot(left, w[rows(f, FB), :], preferred_element_type=F32)
            q = dot_nt(left, b[:, cols(f, FB)])
            total = t if total is None else total + t
            back = q if back is None else back + q
        return total, back

    def step_m(k):
        kk = k // parts
        active = mine(k)
        wait(g.at[k, 0, pl.ds(0, 2)], r_y.at[k])
        send(g.at[k, core], g.at[k, core], s_c.at[k], r_c.at[k], dev(dp=d + 1 - 2 * core))
        total, back = half(k, core)
        pacc[...] = total
        bacc[...] = back
        wait(g.at[k, 0], r_c.at[k])
        total, back = half(k, 1 - core)
        back = bacc[...] + back
        bacc[...] = back

        @pl.when(active)
        def _():
            bx[x, kk] = bacc[rows(y * OWNERS + place, T), :]
            for j in range(1, X):
                send(bx.at[x, kk], bx.at[x, kk], s_b.at[kk], r_one.at[5], dev(tensor=(x + j) % X))

        first = (k % parts) * OWNERS
        spread = se[:, pl.ds(first, OWNERS), rows(kk, T), :].reshape(Y * OWNERS * T, R)
        weighted = (back * spread).astype(BF)
        pacc[...] += total + dot_nt(weighted, ai[...])

        @pl.when(same)
        def _():
            pacc[...] += g[k, core, :, zh].reshape(Y * OWNERS * T, FB).astype(F32)

        pb[k] = pacc[...].astype(BF).reshape(Y, OWNERS, T, FB)
        for j in range(1, X):
            r = (x + j) % X
            send(pb.at[k, r], rx.at[k, x], s_x.at[k], r_x.at[k], dev(tensor=r))
        own[k] = pacc[rows(x, OWNERS * T), :]

        @pl.when(jnp.logical_and(active, sec < S - 1))
        def _():
            for c in range(2):
                for zz in range(2):
                    send(g.at[k, c, y, zz, place], out.at[kk, c, zz], s_o.at[kk], r_one.at[4], dev(section=sec + 1))

    def step_x(k):
        kk = k // parts
        wait(rx.at[k, pl.ds(0, X - 1)], r_x.at[k])
        total = own[k]
        for j in range(1, X):
            total = total + rx[k, (x + j) % X].reshape(OWNERS * T, FB).astype(F32)
        sp[k] = total.astype(BF).reshape(OWNERS, T, FB)

        @pl.when(sec > 0)
        def _():
            send(sp.at[k], g.at[k, core, x, zh], s_p.at[k], r_s.at[k],
                 dev(dp=x * SUBS + m, section=sec - 1, tensor=y))

        @pl.when(bottom)
        def _():
            for o in range(OWNERS):
                owner = (k % parts) * OWNERS + o
                here = jnp.logical_and(same, m == owner)

                @pl.when(here)
                def _():
                    pltpu.make_async_copy(sp.at[k, o], out.at[kk, core, zh], r_one.at[4]).start()

                @pl.when(jnp.logical_not(here))
                def _():
                    send(sp.at[k, o], out.at[kk, core, zh], s_p.at[k], r_one.at[4],
                         dev(dp=x * SUBS + owner, tensor=y))

    NK = N // parts
    tokens = NK * T
    FD = hl.shape[2]

    def scalings():
        wait(bx.at[pl.ds(0, X - 1)], r_one.at[5])
        wait(dx.at[pl.ds(0, X - 1)], r_one.at[3])
        back = bx[0].reshape(tokens, R)
        down = dx[0]
        for j in range(1, X):
            back = back + bx[j].reshape(tokens, R)
            down = down + dx[j]
        product = down * back
        expert = lax.broadcasted_iota(jnp.int32, (ex, R), 0)
        column = lax.broadcasted_iota(jnp.int32, (ex, R), 1)
        group = jnp.where(expert == lax.div(column, rank), 1.0, 0.0).astype(F32)
        turned = dot_nt(group, product, lax.Precision.HIGHEST)
        sga[sec] = turned
        for j in range(1, S):
            send(sga.at[sec], sga.at[sec], s_one.at[5], r_one.at[6], dev(section=(sec + j) % S))
        per = tokens // mix.shape[0]
        for i in range(mix.shape[0]):
            scale[i] = turned[:, i * per:(i + 1) * per]

        wait(states, l_one.at[5])
        t_hi = turned.astype(BF)
        t_lo = (turned - t_hi.astype(F32)).astype(BF)
        sums = (jnp.dot(t_hi, states[...], preferred_element_type=F32)
                + jnp.dot(t_lo, states[...], preferred_element_type=F32))
        for e in range(DP):
            hl[e] = sums[:, e * FD:(e + 1) * FD].astype(BF)
        for j in range(1, DP):
            e = (d + j) % DP
            send(hl.at[e], hx.at[d], s_one.at[6], r_one.at[7], dev(dp=e))
        hx[d] = hl[d]

    steps = {"S": step_s, "Z": step_z, "R": step_r, "M": step_m, "X": step_x}
    behind = dict(ORDER)

    turns = N + max(behind.values())

    @pl.loop(0, turns + 1)
    def _(i):
        @pl.when(i == jnp.where(top, behind["M"], 0))
        def _():
            prepare()

        @pl.when(i == jnp.where(bottom, N + behind["M"], turns))
        def _():
            scalings()

        for name, lag in ORDER:
            @pl.when(jnp.logical_and(i >= lag, i < N + lag))
            def _():
                steps[name](i - lag)

    wait(hx.at[pl.ds(0, DP - 1)], r_one.at[7])
    total = hx[0].astype(F32)
    for j in range(1, DP):
        total = total + hx[j].astype(F32)
    hg[d] = (total * (1.0 / math.sqrt(tokens * DP))).astype(BF)
    for j in range(1, DP):
        send(hg.at[d], hg.at[d], s_one.at[7], r_one.at[8], dev(dp=(d + j) % DP))

    wait(cta, r_one.at[2])
    wait(sga.at[pl.ds(0, S - 1)], r_one.at[6])
    left = sga[...].reshape(S * ex, tokens).T
    right = cta[...].reshape(S * ex, -1)
    hidden[...] = jnp.dot(left, right, precision=lax.Precision.HIGHEST, preferred_element_type=F32)

    wait(hx.at[pl.ds(0, DP - 1)], r_one.at[8])
    for e in range(DP):
        head[:, e * FD:(e + 1) * FD] = hg[e].astype(F32)
    wait(out, r_one.at[4])
    for f in range(SUBS):
        grads[:, :, f * FB:(f + 1) * FB] = out[:, f % 2, f // 2]
    wait(sall.at[pl.ds(0, DP - 1)], s_one.at[0])

    @pl.when(apart)
    def _():
        wait(ai, s_one.at[1])

    wait(cta.at[pl.ds(0, S - 1)], s_one.at[2])
    wait(dx.at[pl.ds(0, X - 1)], s_one.at[3])
    wait(sga.at[pl.ds(0, S - 1)], s_one.at[5])
    wait(hx.at[pl.ds(0, DP - 1)], s_one.at[6])
    wait(hx.at[pl.ds(0, DP - 1)], s_one.at[7])

    @pl.loop(0, N)
    def _(k):
        kk = k // parts
        wait(g.at[k, 0, pl.ds(0, Y - 1), 0], s_s.at[k])
        wait(g.at[k, 0, 0, 0], s_r.at[k])
        wait(g.at[k, 0, pl.ds(0, Y - 1), 0], s_z.at[k])
        wait(g.at[k, 0], s_c.at[k])
        wait(rx.at[k, pl.ds(0, X - 1)], s_x.at[k])
        active = mine(k)

        @pl.when(active)
        def _():
            wait(bx.at[pl.ds(0, X - 1), kk], s_b.at[kk])

            @pl.when(top)
            def _():
                wait(out.at[kk, 0, pl.ds(0, 1)], s_u.at[k])
                wait(out.at[kk, 1], s_u.at[k])

            @pl.when(sec < S - 1)
            def _():
                wait(out.at[kk], s_o.at[kk])

        local = jnp.logical_and(jnp.logical_and(bottom, same), active)

        @pl.when(local)
        def _():
            if OWNERS > 1:
                wait(sp.at[k, pl.ds(0, OWNERS - 1)], s_p.at[k])

        @pl.when(jnp.logical_not(local))
        def _():
            wait(sp.at[k], s_p.at[k])


def finish(*refs):
    copies = [pltpu.make_async_copy(refs[i], refs[4 + i], refs[8].at[i]) for i in range(4)]
    for copy in copies:
        copy.start()
    for copy in copies:
        copy.wait()


def on_device(u, saved, w, a, b, mix, states, classifier):
    X, S, DP = (lax.axis_size(n) for n in ("tensor", "section", "dp"))
    Y = DP // SUBS
    micro, per, F = u.shape
    T = TOK
    tokens = micro * per
    NK = tokens // T
    N = NK * (SUBS // OWNERS)
    FB = w.shape[2]
    R = a.shape[2]
    ex = mix.shape[2]
    vmem = pl.BlockSpec(memory_space=pltpu.VMEM)
    far = pl.BlockSpec(memory_space=pltpu.HBM)
    dma = pltpu.SemaphoreType.DMA
    sizes = (X, Y, S, DP, N, R)
    shapes = (
        jax.ShapeDtypeStruct((NK, T, F), BF),
        jax.ShapeDtypeStruct((micro, ex, per), F32),
        jax.ShapeDtypeStruct((ex, F), F32),
        jax.ShapeDtypeStruct((tokens, F), F32),
    )
    results = pl.pallas_call(
        functools.partial(kernel, sizes),
        out_shape=shapes,
        in_specs=[far] * 8,
        out_specs=(vmem,) * 4,
        scratch_shapes=[
            pltpu.VMEM((NK, 2, 2, T, FB), BF),
            pltpu.VMEM((NK, T, F), BF),
            pltpu.VMEM((NK, SUBS, T, FB), BF),
            pltpu.VMEM((tokens, F), BF),
            pltpu.VMEM((F, FB), BF),
            pltpu.VMEM((F, R), BF),
            pltpu.VMEM((R, F), BF),
            pltpu.VMEM((micro, ex, per), F32),
            pltpu.VMEM((tokens, F), BF),
            pltpu.VMEM((N, 2, Y, 2, OWNERS, T, FB), BF),
            pltpu.VMEM((N, Y, OWNERS, T, FB), BF),
            pltpu.VMEM((N, X, OWNERS, T, FB), BF),
            pltpu.VMEM((N, OWNERS * T, FB), F32),
            pltpu.VMEM((N, OWNERS, T, FB), BF),
            pltpu.VMEM((Y, SUBS, tokens, R), F32),
            pltpu.VMEM((2 * ex, tokens), BF),
            pltpu.VMEM((DP, 2 * ex, tokens), BF),
            pltpu.VMEM((FB, R), BF),
            pltpu.VMEM((X, tokens, R), F32),
            pltpu.VMEM((X, NK, T, R), F32),
            pltpu.VMEM((Y * OWNERS * T, FB), F32),
            pltpu.VMEM((Y * OWNERS * T, R), F32),
            pltpu.VMEM((S, ex, F), F32),
            pltpu.VMEM((S, ex, tokens), F32),
            pltpu.VMEM((DP, ex, F // DP), BF),
            pltpu.VMEM((DP, ex, F // DP), BF),
            pltpu.VMEM((DP, ex, F // DP), BF),
        ] + [dma((N,))] * 16 + [dma((9,)), dma((8,)), dma((7,))],
        compiler_params=pltpu.CompilerParams(
            collective_id=0, has_side_effects=True, vmem_limit_bytes=60 * 1024 * 1024,
        ),
    )(
        u.reshape(NK, T, F),
        saved.reshape(tokens, F),
        w[0], a[0], b[0],
        mix.transpose(0, 2, 1),
        states.reshape(tokens, F),
        classifier.T,
    )
    grads, scale, head, hidden = pl.pallas_call(
        finish,
        out_shape=shapes,
        in_specs=[vmem] * 4,
        out_specs=(far,) * 4,
        scratch_shapes=[dma((4,))],
    )(*results)
    grads = grads.reshape(1, micro, per, F)
    return grads, scale.transpose(0, 2, 1), head.T, hidden.reshape(micro, per, F)


def solution(mesh):
    return jax.shard_map(
        on_device,
        mesh=mesh,
        in_specs=(
            P(None, "dp", "tensor"),
            P("section", None, "dp", "tensor"),
            P("section", "tensor", "dp"),
            P("section", "tensor", None),
            P("section", None, "tensor"),
            P(None, "dp", "section"),
            P(None, "dp", "tensor"),
            P("tensor", "section"),
        ),
        out_specs=(
            P("section", None, "dp", "tensor"),
            P(None, "dp", "section"),
            P("tensor", "section"),
            P(None, "dp", "tensor"),
        ),
        check_vma=False,
    )
```

```python
import functools
import math

import jax
import jax.numpy as jnp
from jax import lax
from jax.experimental import pallas as pl
from jax.experimental.pallas import tpu as pltpu
from jax.sharding import PartitionSpec as P

BF = jnp.bfloat16
F32 = jnp.float32
NT_DIMS = (((1,), (1,)), ((), ()))
SUBS = 4
TOK = 16
OWNERS = 2
ORDER = (("S", 0), ("M", 3), ("R", 1), ("Z", 1), ("X", 4))


def dot_nt(a, b, precision=None):
    return lax.dot_general(a, b, NT_DIMS, precision=precision, preferred_element_type=F32)


def kernel(
    sizes,
    u, hid_in, w_in, a_in, b_in, mix_in, states_in, ct,
    grads, scale, head, hidden,
    out, uv, us, hid, w, a, b, mix, states,
    g, pb, rx, own, sp, se, sb, sall, ai, dx, bx, pacc, bacc, cta, sga, hl, hx, hg,
    r_s, r_z, r_y, r_c, r_x, r_p, r_n,
    s_s, s_z, s_c, s_x, s_p, s_o, s_b, s_u, s_r,
    r_one, s_one, l_one,
):
    X, Y, S, DP, N, R = sizes
    T = TOK
    FB = w.shape[1]
    ex = mix.shape[1]
    rank = R // ex
    parts = SUBS // OWNERS
    d = lax.axis_index("dp")
    sec = lax.axis_index("section")
    x = lax.axis_index("tensor")
    y = d // SUBS
    m = d % SUBS
    zh = m // 2
    core = m % 2
    place = m % OWNERS

    def dev(dp=None, section=None, tensor=None):
        return {
            "dp": d if dp is None else dp,
            "section": sec if section is None else section,
            "tensor": x if tensor is None else tensor,
        }

    def send(src, dst, ssem, rsem, target):
        pltpu.make_async_remote_copy(
            src_ref=src, dst_ref=dst, send_sem=ssem, recv_sem=rsem,
            device_id=target, device_id_type=pl.DeviceIdType.MESH,
        ).start()

    def wait(ref, sem):
        pltpu.make_async_copy(ref, ref, sem).wait()

    def cols(index, width):
        return pl.ds(pl.multiple_of(index * width, 128), width)

    def rows(index, height):
        return pl.ds(pl.multiple_of(index * height, 16), height)

    def mine(k):
        return m // OWNERS == k % parts

    same = x == y
    apart = jnp.logical_not(same)
    top = sec == S - 1
    bottom = sec == 0

    @pl.when(top)
    def _():
        pltpu.make_async_copy(u, uv, l_one.at[6]).start()

    loads = ((mix_in, mix), (w_in, w), (b_in, b), (hid_in, hid), (a_in, a), (states_in, states))
    for i, (far, near) in enumerate(loads):
        pltpu.make_async_copy(far, near, l_one.at[i]).start()

    barrier = pltpu.get_barrier_semaphore()

    def hello(target):
        pl.semaphore_signal(barrier, inc=1, device_id=target, device_id_type=pl.DeviceIdType.MESH)

    for j in range(1, DP):
        hello(dev(dp=(d + j) % DP))
    for j in range(1, X):
        hello(dev(tensor=(x + j) % X))
    for j in range(1, S):
        hello(dev(section=(sec + j) % S))

    @pl.when(apart)
    def _():
        for o in range(SUBS):
            hello(dev(dp=x * SUBS + o, tensor=y))

        @pl.when(sec > 0)
        def _():
            hello(dev(dp=x * SUBS + m, section=sec - 1, tensor=y))

        @pl.when(sec < S - 1)
        def _():
            hello(dev(dp=x * SUBS + m, section=sec + 1, tensor=y))

    extra = SUBS + jnp.where(bottom, 0, 1) + jnp.where(top, 0, 1)
    pl.semaphore_wait(barrier, DP - 1 + X - 1 + S - 1 + jnp.where(same, 0, extra))

    @pl.when(top)
    def _():
        wait(uv, l_one.at[6])

        @pl.loop(0, N // parts)
        def _(kk):
            k = kk * parts + m // OWNERS
            for o in range(SUBS):
                us[kk, o] = uv[kk, :, o * FB:(o + 1) * FB]
            pltpu.make_async_copy(us.at[kk, m], g.at[k, core, y, zh, place], r_s.at[k]).start()
            for j in range(1, SUBS):
                o = (m + j) % SUBS
                send(us.at[kk, o], g.at[k, o % 2, y, o // 2, place],
                     s_u.at[k], r_s.at[k], dev(dp=y * SUBS + o))

    wait(mix, l_one.at[0])
    s_full = jnp.concatenate([mix[i] for i in range(mix.shape[0])], axis=1)
    s_hi = s_full.astype(BF)
    s_lo = (s_full - s_hi.astype(F32)).astype(BF)
    both = jnp.concatenate([s_hi, s_lo], axis=0)
    sb[...] = both
    sall[d] = both
    for j in range(1, DP):
        send(sb, sall.at[d], s_one.at[0], r_one.at[0], dev(dp=(d + j) % DP))

    @pl.when(apart)
    def _():
        send(a_in.at[rows(m, FB)], ai, s_one.at[1], r_one.at[1], dev(dp=x * SUBS + m, tensor=y))

    @pl.when(same)
    def _():
        pltpu.make_async_copy(a_in.at[rows(m, FB)], ai, r_one.at[1]).start()

    pltpu.make_async_copy(ct, cta.at[sec], r_one.at[2]).start()
    for j in range(1, S):
        send(ct, cta.at[sec], s_one.at[2], r_one.at[2], dev(section=(sec + j) % S))

    def step_s(k):
        block = g.at[k, core, y, zh]
        wait(block, r_s.at[k])
        send(block, block, s_s.at[k], r_z.at[k], dev(dp=(d + 2) % SUBS + y * SUBS))
        send(block, block, s_s.at[k], r_p.at[k], dev(dp=((y + 1) % Y) * SUBS + m))
        send(block, block, s_s.at[k], r_n.at[k], dev(dp=((y + Y - 1) % Y) * SUBS + m))

    def step_r(k):
        before = (y + Y - 1) % Y
        after = (y + 1) % Y
        half = OWNERS // 2
        wait(g.at[k, core, before, zh], r_p.at[k])
        lower = g.at[k, core, before, zh, pl.ds(0, half)]
        send(lower, lower, s_r.at[k], r_y.at[k], dev(dp=after * SUBS + m))
        wait(g.at[k, core, after, zh], r_n.at[k])
        upper = g.at[k, core, after, zh, pl.ds(half, half)]
        send(upper, upper, s_r.at[k], r_y.at[k], dev(dp=before * SUBS + m))

    def step_z(k):
        block = g.at[k, core, y, 1 - zh]
        wait(block, r_z.at[k])
        for j in (2, 1, 3):
            send(block, block, s_z.at[k], r_y.at[k], dev(dp=((y + j) % Y) * SUBS + m))

    def prepare():
        wait(hid, l_one.at[3])
        wait(a, l_one.at[4])
        down = jnp.dot(hid[...], a[...], preferred_element_type=F32)
        dx[x] = down
        for j in range(1, X):
            send(dx.at[x], dx.at[x], s_one.at[3], r_one.at[3], dev(tensor=(x + j) % X))
        wait(sall.at[pl.ds(0, DP - 1)], r_one.at[0])
        expert = lax.broadcasted_iota(jnp.int32, (2 * ex, R), 0)
        column = lax.broadcasted_iota(jnp.int32, (2 * ex, R), 1)
        expand = jnp.where(lax.rem(expert, ex) == lax.div(column, rank), 1.0, 0.0).astype(BF)

        @pl.loop(0, DP)
        def _(owner):
            turned = sall[owner].astype(F32).T.astype(BF)
            se[owner // SUBS, owner % SUBS] = jnp.dot(turned, expand, preferred_element_type=F32)

        wait(ai, r_one.at[1])
        wait(w, l_one.at[1])
        wait(b, l_one.at[2])

    def half(k, c):
        total = None
        back = None
        for zz in range(2):
            f = zz * 2 + c
            left = g[k, c, :, zz].reshape(Y * OWNERS * T, FB)
            t = jnp.dot(left, w[rows(f, FB), :], preferred_element_type=F32)
            q = dot_nt(left, b[:, cols(f, FB)])
            total = t if total is None else total + t
            back = q if back is None else back + q
        return total, back

    def step_m(k):
        kk = k // parts
        active = mine(k)
        wait(g.at[k, 0, pl.ds(0, 2)], r_y.at[k])
        send(g.at[k, core], g.at[k, core], s_c.at[k], r_c.at[k], dev(dp=d + 1 - 2 * core))
        total, back = half(k, core)
        pacc[...] = total
        bacc[...] = back
        wait(g.at[k, 0], r_c.at[k])
        total, back = half(k, 1 - core)
        back = bacc[...] + back
        bacc[...] = back

        @pl.when(active)
        def _():
            bx[x, kk] = bacc[rows(y * OWNERS + place, T), :]
            for j in range(1, X):
                send(bx.at[x, kk], bx.at[x, kk], s_b.at[kk], r_one.at[5], dev(tensor=(x + j) % X))

        first = (k % parts) * OWNERS
        spread = se[:, pl.ds(first, OWNERS), rows(kk, T), :].reshape(Y * OWNERS * T, R)
        weighted = (back * spread).astype(BF)
        pacc[...] += total + dot_nt(weighted, ai[...])

        @pl.when(same)
        def _():
            pacc[...] += g[k, core, :, zh].reshape(Y * OWNERS * T, FB).astype(F32)

        pb[k] = pacc[...].astype(BF).reshape(Y, OWNERS, T, FB)
        for j in range(1, X):
            r = (x + j) % X
            send(pb.at[k, r], rx.at[k, x], s_x.at[k], r_x.at[k], dev(tensor=r))
        own[k] = pacc[rows(x, OWNERS * T), :]

        @pl.when(jnp.logical_and(active, sec < S - 1))
        def _():
            for c in range(2):
                for zz in range(2):
                    send(g.at[k, c, y, zz, place], out.at[kk, c, zz], s_o.at[kk], r_one.at[4], dev(section=sec + 1))

    def step_x(k):
        kk = k // parts
        wait(rx.at[k, pl.ds(0, X - 1)], r_x.at[k])
        total = own[k]
        for j in range(1, X):
            total = total + rx[k, (x + j) % X].reshape(OWNERS * T, FB).astype(F32)
        sp[k] = total.astype(BF).reshape(OWNERS, T, FB)

        @pl.when(sec > 0)
        def _():
            send(sp.at[k], g.at[k, core, x, zh], s_p.at[k], r_s.at[k],
                 dev(dp=x * SUBS + m, section=sec - 1, tensor=y))

        @pl.when(bottom)
        def _():
            for o in range(OWNERS):
                owner = (k % parts) * OWNERS + o
                here = jnp.logical_and(same, m == owner)

                @pl.when(here)
                def _():
                    pltpu.make_async_copy(sp.at[k, o], out.at[kk, core, zh], r_one.at[4]).start()

                @pl.when(jnp.logical_not(here))
                def _():
                    send(sp.at[k, o], out.at[kk, core, zh], s_p.at[k], r_one.at[4],
                         dev(dp=x * SUBS + owner, tensor=y))

    NK = N // parts
    tokens = NK * T
    FD = hl.shape[2]

    def scalings():
        wait(bx.at[pl.ds(0, X - 1)], r_one.at[5])
        wait(dx.at[pl.ds(0, X - 1)], r_one.at[3])
        back = bx[0].reshape(tokens, R)
        down = dx[0]
        for j in range(1, X):
            back = back + bx[j].reshape(tokens, R)
            down = down + dx[j]
        product = down * back
        expert = lax.broadcasted_iota(jnp.int32, (ex, R), 0)
        column = lax.broadcasted_iota(jnp.int32, (ex, R), 1)
        group = jnp.where(expert == lax.div(column, rank), 1.0, 0.0).astype(F32)
        turned = dot_nt(group, product, lax.Precision.HIGHEST)
        sga[sec] = turned
        for j in range(1, S):
            send(sga.at[sec], sga.at[sec], s_one.at[5], r_one.at[6], dev(section=(sec + j) % S))
        per = tokens // mix.shape[0]
        for i in range(mix.shape[0]):
            scale[i] = turned[:, i * per:(i + 1) * per]

        wait(states, l_one.at[5])
        t_hi = turned.astype(BF)
        t_lo = (turned - t_hi.astype(F32)).astype(BF)
        sums = (jnp.dot(t_hi, states[...], preferred_element_type=F32)
                + jnp.dot(t_lo, states[...], preferred_element_type=F32))
        for e in range(DP):
            hl[e] = sums[:, e * FD:(e + 1) * FD].astype(BF)
        for j in range(1, DP):
            e = (d + j) % DP
            send(hl.at[e], hx.at[d], s_one.at[6], r_one.at[7], dev(dp=e))
        hx[d] = hl[d]

    steps = {"S": step_s, "Z": step_z, "R": step_r, "M": step_m, "X": step_x}
    behind = dict(ORDER)

    turns = N + max(behind.values())

    @pl.loop(0, turns + 1)
    def _(i):
        @pl.when(i == jnp.where(top, behind["M"], 0))
        def _():
            prepare()

        @pl.when(i == jnp.where(bottom, N + behind["M"], turns))
        def _():
            scalings()

        for name, lag in ORDER:
            @pl.when(jnp.logical_and(i >= lag, i < N + lag))
            def _():
                steps[name](i - lag)

    wait(hx.at[pl.ds(0, DP - 1)], r_one.at[7])
    total = hx[0].astype(F32)
    for j in range(1, DP):
        total = total + hx[j].astype(F32)
    hg[d] = (total * (1.0 / math.sqrt(tokens * DP))).astype(BF)
    for j in range(1, DP):
        send(hg.at[d], hg.at[d], s_one.at[7], r_one.at[8], dev(dp=(d + j) % DP))

    wait(cta, r_one.at[2])
    wait(sga.at[pl.ds(0, S - 1)], r_one.at[6])
    left = sga[...].reshape(S * ex, tokens).T
    right = cta[...].reshape(S * ex, -1)
    hidden[...] = jnp.dot(left, right, precision=lax.Precision.HIGHEST, preferred_element_type=F32)

    wait(out, r_one.at[4])
    for f in range(SUBS):
        grads[:, :, f * FB:(f + 1) * FB] = out[:, f % 2, f // 2]

    wait(hx.at[pl.ds(0, DP - 1)], r_one.at[8])
    for e in range(DP):
        head[:, e * FD:(e + 1) * FD] = hg[e].astype(F32)
    wait(sall.at[pl.ds(0, DP - 1)], s_one.at[0])

    @pl.when(apart)
    def _():
        wait(ai, s_one.at[1])

    wait(cta.at[pl.ds(0, S - 1)], s_one.at[2])
    wait(dx.at[pl.ds(0, X - 1)], s_one.at[3])
    wait(sga.at[pl.ds(0, S - 1)], s_one.at[5])
    wait(hx.at[pl.ds(0, DP - 1)], s_one.at[6])
    wait(hx.at[pl.ds(0, DP - 1)], s_one.at[7])

    @pl.loop(0, N)
    def _(k):
        kk = k // parts
        wait(g.at[k, 0, pl.ds(0, Y - 1), 0], s_s.at[k])
        wait(g.at[k, 0, 0, 0], s_r.at[k])
        wait(g.at[k, 0, pl.ds(0, Y - 1), 0], s_z.at[k])
        wait(g.at[k, 0], s_c.at[k])
        wait(rx.at[k, pl.ds(0, X - 1)], s_x.at[k])
        active = mine(k)

        @pl.when(active)
        def _():
            wait(bx.at[pl.ds(0, X - 1), kk], s_b.at[kk])

            @pl.when(top)
            def _():
                wait(out.at[kk, 0, pl.ds(0, 1)], s_u.at[k])
                wait(out.at[kk, 1], s_u.at[k])

            @pl.when(sec < S - 1)
            def _():
                wait(out.at[kk], s_o.at[kk])

        local = jnp.logical_and(jnp.logical_and(bottom, same), active)

        @pl.when(local)
        def _():
            if OWNERS > 1:
                wait(sp.at[k, pl.ds(0, OWNERS - 1)], s_p.at[k])

        @pl.when(jnp.logical_not(local))
        def _():
            wait(sp.at[k], s_p.at[k])


def finish(*refs):
    copies = [pltpu.make_async_copy(refs[i], refs[4 + i], refs[8].at[i]) for i in range(4)]
    for copy in copies:
        copy.start()
    for copy in copies:
        copy.wait()


def on_device(u, saved, w, a, b, mix, states, classifier):
    X, S, DP = (lax.axis_size(n) for n in ("tensor", "section", "dp"))
    Y = DP // SUBS
    micro, per, F = u.shape
    T = TOK
    tokens = micro * per
    NK = tokens // T
    N = NK * (SUBS // OWNERS)
    FB = w.shape[2]
    R = a.shape[2]
    ex = mix.shape[2]
    vmem = pl.BlockSpec(memory_space=pltpu.VMEM)
    far = pl.BlockSpec(memory_space=pltpu.HBM)
    dma = pltpu.SemaphoreType.DMA
    sizes = (X, Y, S, DP, N, R)
    shapes = (
        jax.ShapeDtypeStruct((NK, T, F), BF),
        jax.ShapeDtypeStruct((micro, ex, per), F32),
        jax.ShapeDtypeStruct((ex, F), F32),
        jax.ShapeDtypeStruct((tokens, F), F32),
    )
    results = pl.pallas_call(
        functools.partial(kernel, sizes),
        out_shape=shapes,
        in_specs=[far] * 8,
        out_specs=(vmem,) * 4,
        scratch_shapes=[
            pltpu.VMEM((NK, 2, 2, T, FB), BF),
            pltpu.VMEM((NK, T, F), BF),
            pltpu.VMEM((NK, SUBS, T, FB), BF),
            pltpu.VMEM((tokens, F), BF),
            pltpu.VMEM((F, FB), BF),
            pltpu.VMEM((F, R), BF),
            pltpu.VMEM((R, F), BF),
            pltpu.VMEM((micro, ex, per), F32),
            pltpu.VMEM((tokens, F), BF),
            pltpu.VMEM((N, 2, Y, 2, OWNERS, T, FB), BF),
            pltpu.VMEM((N, Y, OWNERS, T, FB), BF),
            pltpu.VMEM((N, X, OWNERS, T, FB), BF),
            pltpu.VMEM((N, OWNERS * T, FB), F32),
            pltpu.VMEM((N, OWNERS, T, FB), BF),
            pltpu.VMEM((Y, SUBS, tokens, R), F32),
            pltpu.VMEM((2 * ex, tokens), BF),
            pltpu.VMEM((DP, 2 * ex, tokens), BF),
            pltpu.VMEM((FB, R), BF),
            pltpu.VMEM((X, tokens, R), F32),
            pltpu.VMEM((X, NK, T, R), F32),
            pltpu.VMEM((Y * OWNERS * T, FB), F32),
            pltpu.VMEM((Y * OWNERS * T, R), F32),
            pltpu.VMEM((S, ex, F), F32),
            pltpu.VMEM((S, ex, tokens), F32),
            pltpu.VMEM((DP, ex, F // DP), BF),
            pltpu.VMEM((DP, ex, F // DP), BF),
            pltpu.VMEM((DP, ex, F // DP), BF),
        ] + [dma((N,))] * 16 + [dma((9,)), dma((8,)), dma((7,))],
        compiler_params=pltpu.CompilerParams(
            collective_id=0, has_side_effects=True, vmem_limit_bytes=60 * 1024 * 1024,
        ),
    )(
        u.reshape(NK, T, F),
        saved.reshape(tokens, F),
        w[0], a[0], b[0],
        mix.transpose(0, 2, 1),
        states.reshape(tokens, F),
        classifier.T,
    )
    grads, scale, head, hidden = pl.pallas_call(
        finish,
        out_shape=shapes,
        in_specs=[vmem] * 4,
        out_specs=(far,) * 4,
        scratch_shapes=[dma((4,))],
    )(*results)
    grads = grads.reshape(1, micro, per, F)
    return grads, scale.transpose(0, 2, 1), head.T, hidden.reshape(micro, per, F)


def solution(mesh):
    return jax.shard_map(
        on_device,
        mesh=mesh,
        in_specs=(
            P(None, "dp", "tensor"),
            P("section", None, "dp", "tensor"),
            P("section", "tensor", "dp"),
            P("section", "tensor", None),
            P("section", None, "tensor"),
            P(None, "dp", "section"),
            P(None, "dp", "tensor"),
            P("tensor", "section"),
        ),
        out_specs=(
            P("section", None, "dp", "tensor"),
            P(None, "dp", "section"),
            P("tensor", "section"),
            P(None, "dp", "tensor"),
        ),
        check_vma=False,
    )
```
